256 devices in a mesh: blk: 16 (over y_hi, z), frames: 16 (over x, y_lo, core).
Axes of the slice: x: 4, y: 4 (y_hi: 2, y_lo: 2; y = y_hi * 2 + y_lo), z: 8, core: 2. Of those that a mesh axis runs over, the one named last changes fastest.
Arguments:
- coarse_query: bfloat16 [512, 16, 256], P('blk'), may hold values from -125 to 125
- coarse_feat: bfloat16 [64, 8160, 256], P('frames', 'blk'), may hold values from -61 to 61
- fine_query: bfloat16 [512, 128], P(('blk', 'frames')), may hold values from -175 to 175
- fine_tiles: bfloat16 [64, 1024, 64, 128], P('frames', 'blk'), may hold values from -61 to 61
- track_pos: int32 [2, 64, 512], P(None, None, ('blk', 'frames')), may hold values from 0 to 959, as said below
- tile_list: int32 [64, 16, 16, 8], P('frames', 'blk'), may hold values from 0 to 63, as said below
- tile_valid: int32 [64, 16, 16, 8], P('frames', 'blk'), may hold values from 0 to 1, as said below
Outputs:
- coarse_pos: float32 [2, 64, 512], P(None, 'frames', 'blk')
- fine_offset: float32 [2, 64, 512], P(None, None, ('blk', 'frames'))
The draws below stay inside these ranges and needn't reach their ends.
Inputs may be any that keep to these rules, and one draw needn't show every extreme that they name: `tile_list`: in each list the valid slots come first and name distinct tiles of the group's window; padded slots hold 63; in every frame and group some owner's list is full. `tile_valid`: each list has at least 4 valid slots. `track_pos`: rows lie below 544 and columns below 960.
All inputs are finite; a program needn't handle non-finite values.
Results may differ from the reference program's by a relative error of at most 0.0003.
Values may be sent and summed in bfloat16 or wider, within the bound.
A program may use at most 192 MiB of HBM per device.

```python
import math
import jax
import jax.numpy as jnp
from jax import lax

C = 256
CF = 128
GH = 68
GW = 120
TILE = 8
SUP = 16
CAP = 8
TR_OWN = 2
FT = 64
OWNERS = 16
GROUPS = 16
WIN = 64
TRACKS = 512
POS = 8160
REG = 510
CELLS = 64


def plan_lists(key):
    base_key = jax.random.fold_in(key, 101)
    keys = jax.random.split(base_key, 6)
    starts = jax.random.randint(keys[0], (WIN, GROUPS, OWNERS), 0, FT - 2 * CAP + 1)
    counts = jax.random.randint(keys[1], (WIN, GROUPS, OWNERS), max(CAP // 2, 1), CAP + 1)
    full_owner = jax.random.randint(keys[2], (WIN, GROUPS, 1), 0, OWNERS)
    counts = jnp.where(jnp.arange(OWNERS)[None, None, :] == full_owner, CAP, counts)
    ranks = jax.random.randint(keys[3], (WIN, GROUPS, OWNERS, 2 * CAP), 0, 1 << 20) * (2 * CAP) + jnp.arange(2 * CAP)
    offsets = jnp.argsort(ranks, axis=-1)[..., :CAP].astype(jnp.int32)
    valid = jnp.arange(CAP)[None, None, None, :] < counts[..., None]
    ids = jnp.where(valid, starts[..., None] + offsets, FT - 1).astype(jnp.int32)
    first_cell = jnp.arange(GROUPS)[None, :, None] * REG + starts
    first_row = first_cell // GW * TILE
    first_col = first_cell % GW * TILE
    rows_drawn = jax.random.randint(keys[4], (WIN, GROUPS, OWNERS, TR_OWN), 0, 2 * TILE) + first_row[..., None]
    cols_drawn = jax.random.randint(keys[5], (WIN, GROUPS, OWNERS, TR_OWN), 0, 2 * TILE * CAP) + first_col[..., None]
    rows_drawn = jnp.minimum(rows_drawn, TILE * GH - 1)
    cols_drawn = jnp.minimum(cols_drawn, TILE * GW - 1)
    places = jnp.stack([rows_drawn.reshape(WIN, TRACKS), cols_drawn.reshape(WIN, TRACKS)]).astype(jnp.int32)
    return (ids, valid.astype(jnp.int32), places)


def coarse_pair(key):
    base_key = jax.random.fold_in(key, 202)
    keys = jax.random.split(base_key, 2)
    feats = jnp.clip(jax.random.normal(keys[0], (WIN, POS, C), jnp.float32), -6.0, 6.0)
    queries = jnp.clip(jax.random.normal(keys[1], (TRACKS, SUP, C), jnp.float32), -6.0, 6.0)
    return (feats, queries)


def fine_pair(key):
    base_key = jax.random.fold_in(key, 303)
    keys = jax.random.split(base_key, 2)
    tiles = jnp.clip(jax.random.normal(keys[0], (WIN, GROUPS * FT, CELLS, CF), jnp.float32), -6.0, 6.0)
    descs = jnp.clip(jax.random.normal(keys[1], (TRACKS, CF), jnp.float32), -6.0, 6.0)
    return (tiles, descs)


def draw_coarse_query(key, part):
    return coarse_pair(key)[1].astype(jnp.bfloat16)


def draw_coarse_feat(key, part):
    return coarse_pair(key)[0].astype(jnp.bfloat16)


def draw_fine_query(key, part):
    return fine_pair(key)[1].astype(jnp.bfloat16)


def draw_fine_tiles(key, part):
    return fine_pair(key)[0].astype(jnp.bfloat16)


def draw_track_pos(key, part):
    return plan_lists(key)[2]


def draw_tile_list(key, part):
    return plan_lists(key)[0]


def draw_tile_valid(key, part):
    return plan_lists(key)[1]


def setup_inputs(seed: int = 0) -> dict:
    key_list = jax.random.split(jax.random.key(seed), 8)
    coarse_query = draw_coarse_query(jax.random.fold_in(key_list[7], 71), 0)
    coarse_feat = draw_coarse_feat(jax.random.fold_in(key_list[7], 71), 0)
    fine_query = draw_fine_query(jax.random.fold_in(key_list[7], 71), 0)
    fine_tiles = draw_fine_tiles(jax.random.fold_in(key_list[7], 71), 0)
    track_pos = draw_track_pos(jax.random.fold_in(key_list[7], 71), 0)
    tile_list = draw_tile_list(jax.random.fold_in(key_list[7], 71), 0)
    tile_valid = draw_tile_valid(jax.random.fold_in(key_list[7], 71), 0)
    return {"coarse_query": coarse_query, "coarse_feat": coarse_feat, "fine_query": fine_query, "fine_tiles": fine_tiles, "track_pos": track_pos, "tile_list": tile_list, "tile_valid": tile_valid}


spread_cells = 32.0

def refine_frame(descriptors, tile_block, tile_ids, tile_live, track_row, track_col, base_cell):
    slot_count, cell_count, channels = tile_block.shape
    flat_tiles = tile_block.reshape(slot_count * cell_count, channels).astype(jnp.float32)
    scores = jnp.einsum('nc,kc->nk', descriptors.astype(jnp.float32), flat_tiles, precision=lax.Precision.HIGHEST) * (1.0 / math.sqrt(channels))
    global_cell = base_cell + tile_ids.astype(jnp.int32)
    inner_cell = jnp.arange(cell_count, dtype=jnp.int32)
    cell_row = (global_cell // GW * TILE)[:, None] + (inner_cell // TILE)[None, :]
    cell_col = (global_cell % GW * TILE)[:, None] + (inner_cell % TILE)[None, :]
    cell_row = cell_row.reshape(-1).astype(jnp.float32)
    cell_col = cell_col.reshape(-1).astype(jnp.float32)
    distance = (cell_row[None, :] - track_row[:, None]) ** 2 + (cell_col[None, :] - track_col[:, None]) ** 2
    scores = scores - distance * (0.5 / (spread_cells * spread_cells))
    live_cells = jnp.broadcast_to(tile_live[:, None] > 0, (slot_count, cell_count)).reshape(-1)
    scores = jnp.where(live_cells[None, :], scores, -1e+30)
    highest = lax.optimization_barrier(jnp.max(scores, axis=1, keepdims=True))
    weights = jnp.exp(scores - highest)
    totals = lax.optimization_barrier(jnp.sum(weights, axis=1))
    mean_row = lax.optimization_barrier(jnp.sum(weights * cell_row[None, :], axis=1)) / totals
    mean_col = lax.optimization_barrier(jnp.sum(weights * cell_col[None, :], axis=1)) / totals
    return ((mean_row - track_row) / spread_cells, (mean_col - track_col) / spread_cells)

def reference(coarse_query, coarse_feat, fine_query, fine_tiles, track_pos, tile_list, tile_valid):
    track_group = TRACKS // GROUPS
    query_groups = coarse_query.reshape(GROUPS, track_group * SUP, C)
    positions = jnp.arange(POS, dtype=jnp.int32)
    pos_row = (positions // GW).astype(jnp.float32)
    pos_col = (positions % GW).astype(jnp.float32)
    scale = 1.0 / math.sqrt(C)

    def coarse_one(index):
        frame_index = index // GROUPS
        group_index = index % GROUPS
        scores = jnp.dot(query_groups[group_index], coarse_feat[frame_index].T, preferred_element_type=jnp.float32) * scale
        highest = lax.optimization_barrier(jnp.max(scores, axis=1, keepdims=True))
        weights = jnp.exp(scores - highest)
        totals = lax.optimization_barrier(jnp.sum(weights, axis=1))
        row_mean = (lax.optimization_barrier(jnp.sum(weights * pos_row[None, :], axis=1)) / totals).reshape(track_group, SUP).mean(axis=1)
        col_mean = (lax.optimization_barrier(jnp.sum(weights * pos_col[None, :], axis=1)) / totals).reshape(track_group, SUP).mean(axis=1)
        return jnp.stack([(row_mean - (GH - 1) / 2.0) / (GH / 4.0), (col_mean - (GW - 1) / 2.0) / (GW / 4.0)])
    coarse_all = lax.map(coarse_one, jnp.arange(WIN * GROUPS, dtype=jnp.int32))
    coarse_pos = coarse_all.reshape(WIN, GROUPS, 2, track_group).transpose(2, 0, 1, 3).reshape(2, WIN, TRACKS)
    tiles_all = fine_tiles.reshape(WIN, GROUPS, FT, CELLS, CF)
    descs = fine_query.reshape(GROUPS, OWNERS, TR_OWN, CF)
    places = track_pos.astype(jnp.float32).reshape(2, WIN, GROUPS, OWNERS, TR_OWN)
    bases = jnp.arange(GROUPS, dtype=jnp.int32) * REG
    per_owner = jax.vmap(refine_frame, in_axes=(0, 0, 0, 0, 0, 0, None))
    per_group = jax.vmap(per_owner, in_axes=(0, 0, 0, 0, 0, 0, 0))

    def fine_one(frame_index):
        lists = tile_list[frame_index]
        picked = tiles_all[frame_index][jnp.arange(GROUPS, dtype=jnp.int32)[:, None, None], lists]
        rows_out, cols_out = per_group(descs, picked, lists, tile_valid[frame_index], places[0, frame_index], places[1, frame_index], bases)
        return jnp.stack([rows_out, cols_out])
    fine_all = lax.map(fine_one, jnp.arange(WIN, dtype=jnp.int32))
    fine_offset = fine_all.transpose(1, 0, 2, 3, 4).reshape(2, WIN, TRACKS)
    return (coarse_pos, fine_offset)
```

```python
import math

import jax
import jax.numpy as jnp
from jax import lax
from jax.sharding import PartitionSpec as P

GH = 68
GW = 120
TILE = 8
SPREAD = 32.0


def coarse(coarse_query, coarse_feat):
    track_group, heads, channels = coarse_query.shape
    frames_here, region, _ = coarse_feat.shape
    blocks = lax.axis_size("blk")
    scale = 1.0 / math.sqrt(channels)
    start = lax.axis_index("blk") * region
    queries = lax.all_gather(
        coarse_query.reshape(track_group * heads, channels), "blk", axis=0
    )
    positions = start + jnp.arange(region, dtype=jnp.int32)
    pos_row = (positions // GW).astype(jnp.float32)
    pos_col = (positions % GW).astype(jnp.float32)
    scores = (
        jnp.einsum("brc,fpc->bfpr", queries, coarse_feat, preferred_element_type=jnp.float32)
        * scale
    )
    top = jnp.max(scores, axis=2)
    weights = jnp.exp(scores - top[:, :, None])
    stats = jnp.stack(
        [
            top,
            jnp.sum(weights, axis=2),
            jnp.sum(weights * pos_row[None, None, :, None], axis=2),
            jnp.sum(weights * pos_col[None, None, :, None], axis=2),
        ],
        axis=1,
    )
    stats = lax.all_to_all(stats, "blk", split_axis=0, concat_axis=0, tiled=True)
    top = jnp.max(stats[:, 0], axis=0, keepdims=True)
    factor = jnp.exp(stats[:, 0] - top)
    total = jnp.sum(stats[:, 1] * factor, axis=0)
    rows = jnp.sum(stats[:, 2] * factor, axis=0) / total
    cols = jnp.sum(stats[:, 3] * factor, axis=0) / total
    rows = jnp.mean(rows.reshape(frames_here, track_group, heads), axis=2)
    cols = jnp.mean(cols.reshape(frames_here, track_group, heads), axis=2)
    return jnp.stack(
        [(rows - (GH - 1) / 2.0) / (GH / 4.0), (cols - (GW - 1) / 2.0) / (GW / 4.0)]
    )


def fine(fine_query, fine_tiles, track_pos, tile_list, tile_valid, region):
    frames_here, tiles, cells, channels = fine_tiles.shape
    owners = tile_list.shape[2]
    owned = fine_query.shape[0]
    start = lax.axis_index("blk") * region
    descs = lax.all_gather(fine_query, "frames", axis=0, tiled=True)
    places = lax.all_to_all(
        track_pos, "frames", split_axis=1, concat_axis=2, tiled=True
    ).astype(jnp.float32)
    scores = jnp.einsum(
        "nc,fkc->fnk",
        descs,
        fine_tiles.reshape(frames_here, tiles * cells, channels),
        preferred_element_type=jnp.float32,
    ) * (1.0 / math.sqrt(channels))
    ids = tile_list[:, 0]
    live = tile_valid[:, 0]
    listed = jnp.any(
        (ids[:, :, :, None] == jnp.arange(tiles)) & (live[:, :, :, None] > 0), axis=2
    )
    listed = jnp.repeat(jnp.repeat(listed, owned, axis=1), cells, axis=2)
    index = jnp.arange(tiles * cells, dtype=jnp.int32)
    cell = start + index // cells
    inner = index % cells
    row = (cell // GW * TILE + inner // TILE).astype(jnp.float32)
    col = (cell % GW * TILE + inner % TILE).astype(jnp.float32)
    away_row = row - places[0][:, :, None]
    away_col = col - places[1][:, :, None]
    scores = scores - (away_row**2 + away_col**2) * (0.5 / (SPREAD * SPREAD))
    scores = jnp.where(listed, scores, -1e30)
    weights = jnp.exp(scores - jnp.max(scores, axis=2, keepdims=True))
    total = jnp.sum(weights, axis=2)
    out = jnp.stack(
        [
            jnp.sum(weights * away_row, axis=2) / total / SPREAD,
            jnp.sum(weights * away_col, axis=2) / total / SPREAD,
        ]
    )
    return lax.all_to_all(out, "frames", split_axis=2, concat_axis=1, tiled=True)


def body(coarse_query, coarse_feat, fine_query, fine_tiles, track_pos, tile_list, tile_valid):
    offset = fine(
        fine_query, fine_tiles, track_pos, tile_list, tile_valid, coarse_feat.shape[1]
    )
    return (coarse(coarse_query, coarse_feat), offset)


def solution(mesh):
    return jax.shard_map(
        body,
        mesh=mesh,
        in_specs=(
            P("blk", None, None),
            P("frames", "blk", None),
            P(("blk", "frames"), None),
            P("frames", "blk", None, None),
            P(None, None, ("blk", "frames")),
            P("frames", "blk", None, None),
            P("frames", "blk", None, None),
        ),
        out_specs=(P(None, "frames", "blk"), P(None, None, ("blk", "frames"))),
        check_vma=False,
    )
```

```python
import functools
import math

import jax
import jax.numpy as jnp
from jax import lax
from jax.experimental import pallas as pl
from jax.experimental.pallas import tpu as pltpu
from jax.sharding import PartitionSpec as P

GH = 68
GW = 120
TILE = 8
SPREAD = 32.0
NT = (((1,), (1,)), ((), ()))
RING = 8
PEERS = 16
BLOCK = 15
SCALE = math.log2(math.e) / 16.0


def coarse_group(query, feat, first_block):
    rows = query.shape[0]
    sub = lax.broadcasted_iota(jnp.int32, (8, rows), 0)
    odd = (sub >= 4).astype(jnp.float32)
    top = jnp.full((8, rows), -jnp.inf, jnp.float32)
    total = jnp.zeros((8, rows), jnp.float32)
    row_sum = total
    col_sum = total
    for k in range(9):
        runs = 2 if k < 8 else 1
        size = 240 if k < 8 else 128
        scores = lax.dot_general(
            feat[k * 240 : k * 240 + size, :], query, NT, preferred_element_type=jnp.float32
        )
        scores = scores[: runs * BLOCK * 8].reshape(runs * BLOCK, 8, rows)
        new_top = jnp.maximum(top, jnp.max(scores, axis=0))
        keep = jnp.exp2((top - new_top) * SCALE)
        top = new_top
        total = total * keep
        row_sum = row_sum * keep
        col_sum = col_sum * keep
        for h in range(runs):
            run = moment = None
            for a in range(BLOCK - 1, -1, -1):
                weight = jnp.exp2((scores[h * BLOCK + a] - top) * SCALE)
                run = weight if run is None else run + weight
                if a > 0:
                    moment = run if moment is None else moment + run
            block = first_block + (2 * k + h)
            row = (block // 4).astype(jnp.float32) - (GH - 1) / 2.0
            col = ((block % 4) * 30).astype(jnp.float32) - (GW - 1) / 2.0
            total = total + run
            row_sum = row_sum + run * row
            col_sum = col_sum + (run * (col + odd) + 2.0 * moment)
    both = jnp.maximum(top, pltpu.roll(top, 4, 0))
    keep = jnp.exp2((top - both) * SCALE)
    total = total * keep
    row_sum = row_sum * keep
    col_sum = col_sum * keep
    total = total + pltpu.roll(total, 4, 0)
    row_sum = row_sum + pltpu.roll(row_sum, 4, 0)
    col_sum = col_sum + pltpu.roll(col_sum, 4, 0)
    low = sub < 4
    return jnp.where(low, both, total), jnp.where(low, row_sum, col_sum)


def coarse_combine(stats, out):
    rows = stats.shape[-1]
    low = lax.broadcasted_iota(jnp.int32, (8, rows), 0) < 4
    tops = []
    for i in range(PEERS):
        first = stats[i, 0]
        tops.append(jnp.where(low, first, pltpu.roll(first, 4, 0)))
    top = functools.reduce(jnp.maximum, tops)
    total = jnp.zeros((8, rows), jnp.float32)
    sums = total
    for i in range(PEERS):
        factor = jnp.exp2((tops[i] - top) * SCALE)
        total = total + stats[i, 0] * factor
        sums = sums + stats[i, 1] * factor
    total = jnp.where(low, pltpu.roll(total, 4, 0), total)
    mean = sums / total
    head = lax.broadcasted_iota(jnp.int32, (rows, 128), 0) // 16
    track = lax.broadcasted_iota(jnp.int32, (rows, 128), 1)
    pick = (head == track).astype(jnp.float32)
    mean = jnp.dot(
        mean, pick, preferred_element_type=jnp.float32, precision=lax.Precision.HIGHEST
    ) * (1.0 / 16.0)
    out[0] = mean[0:4, 0:32] * (1.0 / (GH / 4.0))
    out[1] = mean[4:8, 0:32] * (1.0 / (GW / 4.0))


def fine_frames(region, blk, frame_block, lists, valid, gathered, tiles, words, place, fscore, reply):
    lane = lax.broadcasted_iota(jnp.int32, (32, 128), 1)
    step = lax.broadcasted_iota(jnp.int32, (32, 128), 0)
    cell = blk * region + 2 * step + (lane >> 6)
    row = (cell * 34953) >> 22
    col = cell - row * GW
    place[0] = (row * TILE + ((lane & 63) >> 3)).astype(jnp.float32)
    place[1] = (col * TILE + (lane & 7)).astype(jnp.float32)
    words[...] = jnp.zeros_like(words)
    ids = lists[...]
    live = valid[...] > 0
    for k in range(4):
        bits = jnp.where(
            jnp.logical_and((ids >> 4) == k, live), jnp.left_shift(1, ids & 15), 0
        ).astype(jnp.float32)
        words[k * 4 : k * 4 + 4, 0:16] = jnp.sum(bits, axis=1)
    by_owner = jnp.transpose(words[...])[0:16]
    by_track = jnp.concatenate([by_owner, by_owner], axis=0)
    descs = jnp.concatenate([gathered[:, 0, :], gathered[:, 1, :]], axis=0).astype(jnp.bfloat16)
    track_row = jnp.concatenate([gathered[:, 2, :], gathered[:, 3, :]], axis=0)
    track_col = jnp.concatenate([gathered[:, 4, :], gathered[:, 5, :]], axis=0)
    right_half = lane >= 64

    def column(array, index):
        picked = jnp.sum(jnp.where(lane == index, array, 0.0), axis=1, keepdims=True)
        return jnp.broadcast_to(picked, (32, 128))

    def frame(w, results):
        at = frame_block * 4 + w
        here_row = column(track_row, at)
        here_col = column(track_col, at)
        masks = []
        for k in range(4):
            word = column(by_track, k * 4 + w).astype(jnp.int32)
            masks.append(jnp.where(right_half, word >> 1, word))
        top = jnp.full((32, 128), -1e30, jnp.float32)
        for q in range(8):
            scores = lax.dot_general(
                descs, tiles[w, q * 512 : q * 512 + 512, :], NT, preferred_element_type=jnp.float32
            ) * (1.0 / math.sqrt(128))
            for h in range(4):
                j = q * 4 + h
                away_row = place[0, j : j + 1, :] - here_row
                away_col = place[1, j : j + 1, :] - here_col
                score = scores[:, h * 128 : h * 128 + 128] - (
                    away_row * away_row + away_col * away_col
                ) * (0.5 / (SPREAD * SPREAD))
                listed = (masks[j // 8] & (1 << (2 * j % 16))) != 0
                score = jnp.where(listed, score, -1e30)
                fscore[j] = score
                top = jnp.maximum(top, score)
        top = jnp.broadcast_to(jnp.max(top, axis=1, keepdims=True), (32, 128))
        total = jnp.zeros((32, 128), jnp.float32)
        row_sum = total
        col_sum = total
        for j in range(32):
            weight = jnp.exp(fscore[j] - top)
            total = total + weight
            row_sum = row_sum + weight * (place[0, j : j + 1, :] - here_row)
            col_sum = col_sum + weight * (place[1, j : j + 1, :] - here_col)
        total = jnp.sum(total, axis=1, keepdims=True)
        row_out = jnp.sum(row_sum, axis=1, keepdims=True) / total * (1.0 / SPREAD)
        col_out = jnp.sum(col_sum, axis=1, keepdims=True) / total * (1.0 / SPREAD)
        here = lane == at
        return (
            jnp.where(here, row_out, results[0]),
            jnp.where(here, col_out, results[1]),
        )

    zeros = jnp.zeros((32, 128), jnp.float32)
    rows, cols = lax.fori_loop(0, 4, frame, (zeros, zeros))
    reply[...] = jnp.zeros_like(reply)
    reply[:, 0, :] = rows[0:16]
    reply[:, 1, :] = rows[16:32]
    reply[:, 2, :] = cols[0:16]
    reply[:, 3, :] = cols[16:32]


def kernel(
    q_in, f_in, tiles_in, desc_in, pos_in, lists, valid,
    coarse_out, fine_out,
    queries, feat, tiles, stats_out, stats_in, note, gathered, reply, answers, words, place, fscore,
    local_sem, y_sem, z_send, z_recv, c_send, c_recv, s_send, s_recv, n_send, n_recv, a_send, a_recv,
):
    blk = lax.axis_index("blk")
    frames = lax.axis_index("frames")
    z = blk % RING
    yh = blk // RING
    core = frames % 2
    half = pl.multiple_of(core * 256, 256)
    cross = {"blk": (1 - yh) * RING + z, "frames": frames + 2 - 4 * ((frames // 2) % 2)}
    sibling = {"blk": blk, "frames": frames + 1 - 2 * core}

    def ring(k):
        return (z + (RING + k)) % RING

    locals_ = [
        pltpu.make_async_copy(q_in, queries.at[z, yh], local_sem.at[0]),
        pltpu.make_async_copy(f_in, feat, local_sem.at[1]),
        pltpu.make_async_copy(tiles_in, tiles, local_sem.at[2]),
    ]
    for c in locals_:
        c.start()

    barrier = pltpu.get_barrier_semaphore()

    def greet(i, _):
        pl.semaphore_signal(barrier, inc=1, device_id={"blk": (blk + i) % PEERS, "frames": frames})
        pl.semaphore_signal(barrier, inc=1, device_id={"blk": blk, "frames": (frames + i) % PEERS})
        return 0

    lax.fori_loop(1, PEERS, greet, 0)
    pl.semaphore_signal(barrier, inc=1, device_id=cross)

    note[...] = jnp.zeros_like(note)
    note[0:2, :] = desc_in[...].astype(jnp.float32)
    note[2:4, 0:64] = pos_in[0].astype(jnp.float32)
    note[4:6, 0:64] = pos_in[1].astype(jnp.float32)
    pl.semaphore_wait(barrier, 2 * (PEERS - 1) + 1)

    def remote(src, dst, send, recv, to):
        return pltpu.make_async_remote_copy(
            src_ref=src, dst_ref=dst, send_sem=send, recv_sem=recv,
            device_id=to, device_id_type=pl.DeviceIdType.MESH,
        )

    own = q_in.at[pl.ds(half, 256)]
    y_copy = remote(own, queries.at[z, yh, pl.ds(half, 256)], y_sem.at[0], y_sem.at[1], cross)

    def z_copy(way, stage):
        to = {"blk": yh * RING + ring(1 - 2 * way), "frames": frames}
        sems = (z_send.at[way, stage], z_recv.at[way, stage])
        if stage == 0:
            return remote(own, queries.at[z, yh, pl.ds(half, 256)], *sems, to)
        if stage == 1:
            ref = queries.at[z, 1 - yh, pl.ds(half, 256)]
        elif stage < 4:
            ref = queries.at[ring((stage - 1) * (2 * way - 1)), :, pl.ds(half, 256)]
        else:
            ref = queries.at[
                ring((stage - 1) * (2 * way - 1)), :, pl.ds(pl.multiple_of(half + 128 * way, 128), 128)
            ]
        return remote(ref, ref, *sems, to)

    def c_copy(k):
        if k == 0:
            ref = queries.at[z, 1 - yh, pl.ds(half, 256)]
        else:
            ref = queries.at[ring({1: -1, 2: -2, 3: -3, 4: 1, 5: 2, 6: 3, 7: -4}[k]), :, pl.ds(half, 256)]
        return remote(ref, ref, c_send.at[k], c_recv.at[k], sibling)

    def note_copy(i):
        return remote(
            note, gathered.at[frames], n_send.at[i], n_recv.at[i],
            {"blk": blk, "frames": (frames + i) % PEERS},
        )

    def answer_copy(i):
        to = (frames + i) % PEERS
        return remote(
            reply.at[to], answers.at[i], a_send.at[i], a_recv.at[i], {"blk": blk, "frames": to}
        )

    def group_of(i):
        j = i - 2
        away = j // 4 + 1
        left = (j % 4) // 2
        shift = jnp.where(i < 2, 0, jnp.where(left == 1, away, -away))
        return (z + RING + shift) % RING, (yh + i) % 2

    def stat_copy(i):
        gz, gy = group_of(i)
        return remote(
            stats_out.at[i], stats_in.at[i], s_send.at[i], s_recv.at[i],
            {"blk": gy * RING + gz, "frames": frames},
        )

    y_copy.start()
    z_copy(0, 0).start()
    z_copy(1, 0).start()

    def start_notes(i, _):
        note_copy(i).start()
        return 0

    lax.fori_loop(1, PEERS, start_notes, 0)
    gathered[frames] = note[...]
    locals_[0].wait()
    locals_[1].wait()

    def fine_stage():
        locals_[2].wait()

        def wait_notes(i, _):
            note_copy(i).wait_recv()
            return 0

        lax.fori_loop(1, PEERS, wait_notes, 0)
        fine_frames(
            510, blk, frames, lists, valid, gathered, tiles, words, place, fscore, reply
        )
        answers[0] = reply[frames]

        def start_answers(i, _):
            answer_copy(i).start()
            return 0

        lax.fori_loop(1, PEERS, start_answers, 0)

    def arrive(stage):
        for way in range(2):
            if stage == 1:
                z_copy(way, 0).wait_recv()
                z_copy(way, 1).wait_recv()
            else:
                z_copy(way, stage).wait_recv()
            if stage < 4:
                z_copy(way, stage + 1).start()
        if stage < 4:
            c_copy(stage).start()
            c_copy(stage + 3).start()
        else:
            c_copy(7).start()

    def group_step(i, _):
        @pl.when(i == 1)
        def _():
            y_copy.wait_recv()
            z_copy(0, 1).start()
            z_copy(1, 1).start()
            c_copy(0).start()
            fine_stage()
            c_copy(0).wait_recv()

        @pl.when(i == 2)
        def _():
            arrive(1)
            c_copy(1).wait_recv()
            c_copy(4).wait_recv()

        @pl.when(i == 5)
        def _():
            arrive(2)

        @pl.when(i == 6)
        def _():
            c_copy(2).wait_recv()
            c_copy(5).wait_recv()

        @pl.when(i == 9)
        def _():
            arrive(3)

        @pl.when(i == 10)
        def _():
            c_copy(3).wait_recv()
            c_copy(6).wait_recv()

        @pl.when(i == 12)
        def _():
            arrive(4)

        @pl.when(i == 14)
        def _():
            c_copy(7).wait_recv()

        gz, gy = group_of(i)
        first, second = coarse_group(queries[gz, gy], feat, blk * 17)

        @pl.when(i == 0)
        def _():
            stats_in[0, 0] = first
            stats_in[0, 1] = second

        @pl.when(i > 0)
        def _():
            stats_out[i, 0] = first
            stats_out[i, 1] = second
            stat_copy(i).start()

        return 0

    lax.fori_loop(0, PEERS, group_step, 0)

    def wait_stats(i, _):
        stat_copy(i).wait_recv()
        answer_copy(i).wait_recv()
        return 0

    lax.fori_loop(1, PEERS, wait_stats, 0)
    coarse_combine(stats_in, coarse_out)
    answer = jnp.sum(answers[...], axis=0)
    fine_out[0] = answer[0:2, 0:64]
    fine_out[1] = answer[2:4, 0:64]

    def wait_sends(i, _):
        stat_copy(i).wait_send()
        answer_copy(i).wait_send()
        note_copy(i).wait_send()
        return 0

    lax.fori_loop(1, PEERS, wait_sends, 0)
    y_copy.wait_send()
    for way in range(2):
        for stage in range(5):
            z_copy(way, stage).wait_send()
    for k in range(8):
        c_copy(k).wait_send()


def body(coarse_query, coarse_feat, fine_query, fine_tiles, track_pos, tile_list, tile_valid):
    track_group, heads, channels = coarse_query.shape
    frames_here, region, _ = coarse_feat.shape
    queries = coarse_query.reshape(track_group * heads, channels)
    feat = jnp.transpose(coarse_feat, (1, 0, 2)).reshape(region * frames_here, channels)
    feat = jnp.pad(feat, ((0, 8), (0, 0)))
    tiles = fine_tiles.reshape(frames_here, -1, fine_tiles.shape[-1])
    pos = jnp.transpose(track_pos, (0, 2, 1))
    lists = jnp.transpose(tile_list[:, 0], (0, 2, 1))
    valid = jnp.transpose(tile_valid[:, 0], (0, 2, 1))
    f32 = jnp.float32
    vmem = pl.BlockSpec(memory_space=pltpu.VMEM)
    far = pl.BlockSpec(memory_space=pl.ANY)
    dma = pltpu.SemaphoreType.DMA
    rows = queries.shape[0]
    coarse_pos, offset = pl.pallas_call(
        kernel,
        out_shape=(
            jax.ShapeDtypeStruct((2, 4, 32), f32),
            jax.ShapeDtypeStruct((2, 2, 64), f32),
        ),
        in_specs=[far, far, far, vmem, vmem, vmem, vmem],
        out_specs=(vmem, vmem),
        scratch_shapes=[
            pltpu.VMEM((RING, 2, rows, channels), jnp.bfloat16),
            pltpu.VMEM(feat.shape, jnp.bfloat16),
            pltpu.VMEM(tiles.shape, jnp.bfloat16),
            pltpu.VMEM((PEERS, 2, 8, rows), f32),
            pltpu.VMEM((PEERS, 2, 8, rows), f32),
            pltpu.VMEM((8, 128), f32),
            pltpu.VMEM((PEERS, 8, 128), f32),
            pltpu.VMEM((PEERS, 8, 128), f32),
            pltpu.VMEM((PEERS, 8, 128), f32),
            pltpu.VMEM((128, 128), f32),
            pltpu.VMEM((2, 32, 128), f32),
            pltpu.VMEM((32, 32, 128), f32),
            dma((3,)),
            dma((2,)),
            dma((2, 5)),
            dma((2, 5)),
            dma((8,)),
            dma((8,)),
            dma((PEERS,)),
            dma((PEERS,)),
            dma((PEERS,)),
            dma((PEERS,)),
            dma((PEERS,)),
            dma((PEERS,)),
        ],
        compiler_params=pltpu.CompilerParams(
            collective_id=0, has_side_effects=True, vmem_limit_bytes=56 * 2**20
        ),
        cost_estimate=pl.CostEstimate(
            flops=2 * 8192 * 2048 * 256, bytes_accessed=6 * 10**6, transcendentals=8192 * 2048
        ),
    )(queries, feat, tiles, fine_query, pos, lists, valid)
    return coarse_pos, jnp.transpose(offset, (0, 2, 1))


def solution(mesh):
    return jax.shard_map(
        body,
        mesh=mesh,
        in_specs=(
            P("blk", None, None),
            P("frames", "blk", None),
            P(("blk", "frames"), None),
            P("frames", "blk", None, None),
            P(None, None, ("blk", "frames")),
            P("frames", "blk", None, None),
            P("frames", "blk", None, None),
        ),
        out_specs=(P(None, "frames", "blk"), P(None, None, ("blk", "frames"))),
        check_vma=False,
    )
```

```python
import functools
import math

import jax
import jax.numpy as jnp
from jax import lax
from jax.experimental import pallas as pl
from jax.experimental.pallas import tpu as pltpu
from jax.sharding import PartitionSpec as P

GH = 68
GW = 120
TILE = 8
SPREAD = 32.0
NT = (((1,), (1,)), ((), ()))
RING = 8
PEERS = 16
BLOCK = 15
ORDER = (
    (0, 0), (1, 0), (0, -1), (0, 1), (0, -2), (0, 2), (1, -1), (1, 1),
    (0, -3), (0, 3), (1, -2), (1, 2), (0, 4), (1, -3), (1, 3), (1, 4),
)
EVENTS = {
    1: (
        ("near", 1, 0), ("near", 1, 1), ("across", 0), ("fine",), ("near", 2, 0), ("near", 2, 1), ("ready", 1, 0),
    ),
    2: (("ready", 0, 1),),
    3: (("near", 3, 0),),
    4: (("near", 3, 1), ("across", 1), ("ready", 0, 2)),
    6: (("ready", 1, 1),),
    7: (("near", 4, 0), ("across", 2)),
    8: (("ready", 0, 3),),
    10: (("across", 3), ("ready", 1, 2)),
    12: (("ready", 0, 4), ("across", 4)),
    13: (("ready", 1, 3),),
    15: (("ready", 1, 4),),
}
SCALE = math.log2(math.e) / 16.0


def coarse_group(query, feat, first_block):
    rows = query.shape[0]
    sub = lax.broadcasted_iota(jnp.int32, (8, rows), 0)
    odd = (sub >= 4).astype(jnp.float32)
    top = jnp.full((8, rows), -jnp.inf, jnp.float32)
    total = jnp.zeros((8, rows), jnp.float32)
    row_sum = total
    col_sum = total
    for k in range(9):
        runs = 2 if k < 8 else 1
        size = 240 if k < 8 else 128
        scores = lax.dot_general(
            feat[k * 240 : k * 240 + size, :], query, NT, preferred_element_type=jnp.float32
        )
        scores = scores[: runs * BLOCK * 8].reshape(runs * BLOCK, 8, rows)
        new_top = jnp.maximum(top, jnp.max(scores, axis=0))
        keep = jnp.exp2((top - new_top) * SCALE)
        top = new_top
        total = total * keep
        row_sum = row_sum * keep
        col_sum = col_sum * keep
        for h in range(runs):
            run = moment = None
            for a in range(BLOCK - 1, -1, -1):
                weight = jnp.exp2((scores[h * BLOCK + a] - top) * SCALE)
                run = weight if run is None else run + weight
                if a > 0:
                    moment = run if moment is None else moment + run
            block = first_block + (2 * k + h)
            row = (block // 4).astype(jnp.float32) - (GH - 1) / 2.0
            col = ((block % 4) * 30).astype(jnp.float32) - (GW - 1) / 2.0
            total = total + run
            row_sum = row_sum + run * row
            col_sum = col_sum + (run * (col + odd) + 2.0 * moment)
    both = jnp.maximum(top, pltpu.roll(top, 4, 0))
    keep = jnp.exp2((top - both) * SCALE)
    total = total * keep
    row_sum = row_sum * keep
    col_sum = col_sum * keep
    total = total + pltpu.roll(total, 4, 0)
    row_sum = row_sum + pltpu.roll(row_sum, 4, 0)
    col_sum = col_sum + pltpu.roll(col_sum, 4, 0)
    low = sub < 4
    return jnp.where(low, both, total), jnp.where(low, row_sum, col_sum)


def coarse_combine(stats, out):
    rows = stats.shape[-1]
    low = lax.broadcasted_iota(jnp.int32, (8, rows), 0) < 4
    tops = []
    for i in range(PEERS):
        first = stats[i, 0]
        tops.append(jnp.where(low, first, pltpu.roll(first, 4, 0)))
    top = functools.reduce(jnp.maximum, tops)
    total = jnp.zeros((8, rows), jnp.float32)
    sums = total
    for i in range(PEERS):
        factor = jnp.exp2((tops[i] - top) * SCALE)
        total = total + stats[i, 0] * factor
        sums = sums + stats[i, 1] * factor
    total = jnp.where(low, pltpu.roll(total, 4, 0), total)
    mean = sums / total
    head = lax.broadcasted_iota(jnp.int32, (rows, 128), 0) // 16
    track = lax.broadcasted_iota(jnp.int32, (rows, 128), 1)
    pick = (head == track).astype(jnp.float32)
    mean = jnp.dot(
        mean, pick, preferred_element_type=jnp.float32, precision=lax.Precision.HIGHEST
    ) * (1.0 / 16.0)
    out[0] = mean[0:4, 0:32] * (1.0 / (GH / 4.0))
    out[1] = mean[4:8, 0:32] * (1.0 / (GW / 4.0))


def fine_frames(region, blk, frame_block, lists, valid, gathered, tiles, words, place, fscore, reply):
    lane = lax.broadcasted_iota(jnp.int32, (32, 128), 1)
    step = lax.broadcasted_iota(jnp.int32, (32, 128), 0)
    cell = blk * region + 2 * step + (lane >> 6)
    row = (cell * 34953) >> 22
    col = cell - row * GW
    place[0] = (row * TILE + ((lane & 63) >> 3)).astype(jnp.float32)
    place[1] = (col * TILE + (lane & 7)).astype(jnp.float32)
    words[...] = jnp.zeros_like(words)
    ids = lists[...]
    live = valid[...] > 0
    for k in range(4):
        bits = jnp.where(
            jnp.logical_and((ids >> 4) == k, live), jnp.left_shift(1, ids & 15), 0
        ).astype(jnp.float32)
        words[k * 4 : k * 4 + 4, 0:16] = jnp.sum(bits, axis=1)
    by_owner = jnp.transpose(words[...])[0:16]
    by_track = jnp.concatenate([by_owner, by_owner], axis=0)
    descs = jnp.concatenate([gathered[:, 0, :], gathered[:, 1, :]], axis=0).astype(jnp.bfloat16)
    track_row = jnp.concatenate([gathered[:, 2, :], gathered[:, 3, :]], axis=0)
    track_col = jnp.concatenate([gathered[:, 4, :], gathered[:, 5, :]], axis=0)
    right_half = lane >= 64

    def column(array, index):
        picked = jnp.sum(jnp.where(lane == index, array, 0.0), axis=1, keepdims=True)
        return jnp.broadcast_to(picked, (32, 128))

    def frame(w, results):
        at = frame_block * 4 + w
        here_row = column(track_row, at)
        here_col = column(track_col, at)
        masks = []
        for k in range(4):
            word = column(by_track, k * 4 + w).astype(jnp.int32)
            masks.append(jnp.where(right_half, word >> 1, word))
        top = jnp.full((32, 128), -1e30, jnp.float32)
        for q in range(8):
            scores = lax.dot_general(
                descs, tiles[w, q * 512 : q * 512 + 512, :], NT, preferred_element_type=jnp.float32
            ) * (1.0 / math.sqrt(128))
            for h in range(4):
                j = q * 4 + h
                away_row = place[0, j : j + 1, :] - here_row
                away_col = place[1, j : j + 1, :] - here_col
                score = scores[:, h * 128 : h * 128 + 128] - (
                    away_row * away_row + away_col * away_col
                ) * (0.5 / (SPREAD * SPREAD))
                listed = (masks[j // 8] & (1 << (2 * j % 16))) != 0
                score = jnp.where(listed, score, -1e30)
                fscore[j] = score
                top = jnp.maximum(top, score)
        top = jnp.broadcast_to(jnp.max(top, axis=1, keepdims=True), (32, 128))
        total = jnp.zeros((32, 128), jnp.float32)
        row_sum = total
        col_sum = total
        for j in range(32):
            weight = jnp.exp(fscore[j] - top)
            total = total + weight
            row_sum = row_sum + weight * (place[0, j : j + 1, :] - here_row)
            col_sum = col_sum + weight * (place[1, j : j + 1, :] - here_col)
        total = jnp.sum(total, axis=1, keepdims=True)
        row_out = jnp.sum(row_sum, axis=1, keepdims=True) / total * (1.0 / SPREAD)
        col_out = jnp.sum(col_sum, axis=1, keepdims=True) / total * (1.0 / SPREAD)
        here = lane == at
        return (
            jnp.where(here, row_out, results[0]),
            jnp.where(here, col_out, results[1]),
        )

    zeros = jnp.zeros((32, 128), jnp.float32)
    rows, cols = lax.fori_loop(0, 4, frame, (zeros, zeros))
    reply[...] = jnp.zeros_like(reply)
    reply[:, 0, :] = rows[0:16]
    reply[:, 1, :] = rows[16:32]
    reply[:, 2, :] = cols[0:16]
    reply[:, 3, :] = cols[16:32]


def kernel(
    q_in, f_in, tiles_in, desc_in, pos_in, lists, valid,
    coarse_out, fine_out,
    queries, feat, tiles, stats_out, stats_in, note, gathered, reply, answers, words, place, fscore,
    local_sem, near_send, y_recv, z_recv, c_recv, far_send, far_recv,
):
    blk = lax.axis_index("blk")
    frames = lax.axis_index("frames")
    z = blk & (RING - 1)
    yh = blk >> 3
    core = frames & 1
    half = pl.multiple_of(core * 256, 256)
    cross = {"blk": (1 - yh) * RING + z, "frames": frames + 2 - 2 * (frames & 2)}
    sibling = {"blk": blk, "frames": frames + 1 - 2 * core}

    def ring(k):
        return (z + (RING + k)) & (RING - 1)

    locals_ = [
        pltpu.make_async_copy(q_in, queries.at[z, yh], local_sem.at[0]),
        pltpu.make_async_copy(f_in, feat, local_sem.at[1]),
        pltpu.make_async_copy(tiles_in, tiles, local_sem.at[2]),
    ]
    for c in locals_:
        c.start()

    barrier = pltpu.get_barrier_semaphore()

    def greet(i, _):
        pl.semaphore_signal(barrier, inc=1, device_id={"blk": (blk + i) & (PEERS - 1), "frames": frames})
        pl.semaphore_signal(barrier, inc=1, device_id={"blk": blk, "frames": (frames + i) & (PEERS - 1)})
        return 0

    lax.fori_loop(1, PEERS, greet, 0)
    pl.semaphore_signal(barrier, inc=1, device_id=cross)

    note[...] = jnp.zeros_like(note)
    note[0:2, :] = desc_in[...].astype(jnp.float32)
    note[2:4, 0:64] = pos_in[0].astype(jnp.float32)
    note[4:6, 0:64] = pos_in[1].astype(jnp.float32)

    def remote(src, dst, send, recv, to):
        return pltpu.make_async_remote_copy(
            src_ref=src, dst_ref=dst, send_sem=send, recv_sem=recv,
            device_id=to, device_id_type=pl.DeviceIdType.MESH,
        )

    own = q_in.at[pl.ds(half, 256)]
    def part(chain, shift, start, size):
        return queries.at[ring(shift), yh if chain == 0 else 1 - yh, pl.ds(start, size)]

    def rows_of(chunk):
        return pl.multiple_of(half + 128 * chunk, 128)

    def z_copy(way, stage, chunk):
        to = {"blk": yh * RING + ring(1 - 2 * way), "frames": frames}
        at = 2 * (stage - 1) + chunk
        dst = part(0, (stage - 1) * (2 * way - 1), rows_of(chunk), 128)
        src = q_in.at[pl.ds(rows_of(chunk), 128)] if stage == 1 else dst
        return remote(src, dst, near_send.at[0], z_recv.at[way, at], to)

    def y_copy(way, stage, chunk):
        if stage == 0:
            return remote(own, part(0, 0, half, 256), near_send.at[1], y_recv.at[0, 8], cross)
        at = 2 * (stage - 1) + chunk
        ref = part(0, stage * (2 * way - 1), rows_of(chunk), 128)
        return remote(ref, ref, near_send.at[1], y_recv.at[way, at], cross)

    def c_copy(chain, way, stage):
        if stage == 0:
            k = 0
        elif stage < 4:
            k = 1 + chain * 6 + way * 3 + stage - 1
        else:
            k = 13 + chain
        ref = part(chain, stage * (2 * way - 1), half, 256)
        return remote(ref, ref, near_send.at[2], c_recv.at[k], sibling)

    Z_PARTS = [(w, d, c) for w in range(2) for d in range(1, 5) for c in range(2) if d < 4 or c == w]

    def note_copy(i):
        return remote(
            note, gathered.at[frames], far_send.at[0], far_recv.at[0],
            {"blk": blk, "frames": (frames + i) & (PEERS - 1)},
        )

    def answer_copy(i):
        to = (frames + i) & (PEERS - 1)
        return remote(
            reply.at[to], answers.at[i], far_send.at[1], far_recv.at[1], {"blk": blk, "frames": to}
        )

    def group_of(i):
        chain = away = i * 0
        for at, (n, k) in enumerate(ORDER):
            chain = jnp.where(i == at, n, chain)
            away = jnp.where(i == at, k, away)
        return (z + RING + away) & (RING - 1), (yh + chain) & 1

    def stat_copy(i):
        gz, gy = group_of(i)
        return remote(
            stats_out.at[i], stats_in.at[i], far_send.at[2], far_recv.at[2],
            {"blk": gy * RING + gz, "frames": frames},
        )

    def wait_all(ref, sem):
        pltpu.make_async_copy(ref, ref, sem).wait()

    def start_notes(i, _):
        note_copy(i).start()
        return 0

    def enter():
        pl.semaphore_wait(barrier, 2 * (PEERS - 1) + 1)
        for chunk in range(2):
            z_copy(0, 1, chunk).start()
            z_copy(1, 1, chunk).start()
        y_copy(0, 0, 0).start()
        lax.fori_loop(1, PEERS, start_notes, 0)
        gathered[frames] = note[...]

    locals_[0].wait()
    locals_[1].wait()

    def fine_stage():
        locals_[2].wait()

        wait_all(gathered.at[1:PEERS], far_recv.at[0])
        fine_frames(
            510, blk, frames, lists, valid, gathered, tiles, words, place, fscore, reply
        )
        answers[0] = reply[frames]

        def start_answers(i, _):
            answer_copy(i).start()
            return 0

        lax.fori_loop(1, PEERS, start_answers, 0)

    def near(stage, chunk):
        for way in range(2):
            if stage == 4:
                chunk = way
            z_copy(way, stage, chunk).wait_recv()
            if stage < 3 or (stage == 3 and chunk == way):
                z_copy(way, stage + 1, chunk).start()
            y_copy(way, stage, chunk).start()
        if stage == 4:
            c_copy(0, 0, 4).start()
        elif chunk == 1:
            c_copy(0, 0, stage).start()
            c_copy(0, 1, stage).start()

    def across(stage):
        if stage == 0:
            y_copy(0, 0, 0).wait_recv()
            c_copy(1, 0, 0).start()
            return
        for way, d, chunk in Z_PARTS:
            if d == stage:
                y_copy(way, d, chunk).wait_recv()
        c_copy(1, 0, stage).start()
        if stage < 4:
            c_copy(1, 1, stage).start()

    def ready(chain, stage):
        c_copy(chain, 0, stage).wait_recv()
        if 0 < stage < 4:
            c_copy(chain, 1, stage).wait_recv()

    def group_step(i, _):
        @pl.when(i == 0)
        def _():
            enter()

        for when, events in EVENTS.items():
            @pl.when(i == when)
            def _(events=events):
                for event, *at in events:
                    {"near": near, "across": across, "ready": ready, "fine": fine_stage}[event](*at)

        gz, gy = group_of(i)
        first, second = coarse_group(queries[gz, gy], feat, blk * 17)

        @pl.when(i == 0)
        def _():
            stats_in[0, 0] = first
            stats_in[0, 1] = second

        @pl.when(i > 0)
        def _():
            stats_out[i, 0] = first
            stats_out[i, 1] = second
            stat_copy(i).start()

        return 0

    lax.fori_loop(0, PEERS, group_step, 0)

    wait_all(answers.at[1:PEERS], far_recv.at[1])
    wait_all(stats_in.at[1:PEERS], far_recv.at[2])
    coarse_combine(stats_in, coarse_out)
    answer = jnp.sum(answers[...], axis=0)
    fine_out[0] = answer[0:2, 0:64]
    fine_out[1] = answer[2:4, 0:64]

    wait_all(gathered.at[1:PEERS], far_send.at[0])
    wait_all(answers.at[1:PEERS], far_send.at[1])
    wait_all(stats_in.at[1:PEERS], far_send.at[2])
    wait_all(queries.at[0:7, 0, 0:256], near_send.at[0])
    wait_all(queries.at[:, 0, 0:256], near_send.at[1])
    wait_all(queries.at[:, 0, 0:480], near_send.at[2])


def body(coarse_query, coarse_feat, fine_query, fine_tiles, track_pos, tile_list, tile_valid):
    track_group, heads, channels = coarse_query.shape
    frames_here, region, _ = coarse_feat.shape
    queries = coarse_query.reshape(track_group * heads, channels)
    feat = jnp.transpose(coarse_feat, (1, 0, 2)).reshape(region * frames_here, channels)
    feat = jnp.pad(feat, ((0, 8), (0, 0)))
    tiles = fine_tiles.reshape(frames_here, -1, fine_tiles.shape[-1])
    pos = jnp.transpose(track_pos, (0, 2, 1))
    lists = jnp.transpose(tile_list[:, 0], (0, 2, 1))
    valid = jnp.transpose(tile_valid[:, 0], (0, 2, 1))
    f32 = jnp.float32
    vmem = pl.BlockSpec(memory_space=pltpu.VMEM)
    far = pl.BlockSpec(memory_space=pl.ANY)
    dma = pltpu.SemaphoreType.DMA
    rows = queries.shape[0]
    coarse_pos, offset = pl.pallas_call(
        kernel,
        out_shape=(
            jax.ShapeDtypeStruct((2, 4, 32), f32),
            jax.ShapeDtypeStruct((2, 2, 64), f32),
        ),
        in_specs=[far, far, far, vmem, vmem, vmem, vmem],
        out_specs=(vmem, vmem),
        scratch_shapes=[
            pltpu.VMEM((RING, 2, rows, channels), jnp.bfloat16),
            pltpu.VMEM(feat.shape, jnp.bfloat16),
            pltpu.VMEM(tiles.shape, jnp.bfloat16),
            pltpu.VMEM((PEERS, 2, 8, rows), f32),
            pltpu.VMEM((PEERS, 2, 8, rows), f32),
            pltpu.VMEM((8, 128), f32),
            pltpu.VMEM((PEERS, 8, 128), f32),
            pltpu.VMEM((PEERS, 8, 128), f32),
            pltpu.VMEM((PEERS, 8, 128), f32),
            pltpu.VMEM((128, 128), f32),
            pltpu.VMEM((2, 32, 128), f32),
            pltpu.VMEM((32, 32, 128), f32),
            dma((3,)),
            dma((3,)),
            dma((2, 9)),
            dma((2, 8)),
            dma((15,)),
            dma((3,)),
            dma((3,)),
        ],
        compiler_params=pltpu.CompilerParams(
            collective_id=0, has_side_effects=True, vmem_limit_bytes=56 * 2**20
        ),
        cost_estimate=pl.CostEstimate(
            flops=2 * 8192 * 2048 * 256, bytes_accessed=6 * 10**6, transcendentals=8192 * 2048
        ),
    )(queries, feat, tiles, fine_query, pos, lists, valid)
    return coarse_pos, jnp.transpose(offset, (0, 2, 1))


def solution(mesh):
    return jax.shard_map(
        body,
        mesh=mesh,
        in_specs=(
            P("blk", None, None),
            P("frames", "blk", None),
            P(("blk", "frames"), None),
            P("frames", "blk", None, None),
            P(None, None, ("blk", "frames")),
            P("frames", "blk", None, None),
            P("frames", "blk", None, None),
        ),
        out_specs=(P(None, "frames", "blk"), P(None, None, ("blk", "frames"))),
        check_vma=False,
    )
```

```python
import functools
import math

import jax
import jax.numpy as jnp
from jax import lax
from jax.experimental import pallas as pl
from jax.experimental.pallas import tpu as pltpu
from jax.sharding import PartitionSpec as P

GH = 68
GW = 120
TILE = 8
SPREAD = 32.0
NT = (((1,), (1,)), ((), ()))
RING = 8
PEERS = 16
BLOCK = 15
ORDER = (
    (0, 0), (1, 0), (0, -1), (0, 1), (0, -2), (0, 2), (1, -1), (1, 1),
    (0, -3), (0, 3), (1, -2), (1, 2), (0, 4), (1, -3), (1, 3), (1, 4),
)
EVENTS = {
    1: (("near", 1, 0), ("note", 1), ("near", 1, 1), ("across", 0), ("ready", 1, 0)),
    2: (("note", 2), ("near", 2, 0), ("near", 2, 1), ("ready", 0, 1)),
    3: (("note", 3),),
    4: (("near", 3, 0), ("near", 3, 1), ("across", 1), ("ready", 0, 2)),
    5: (("fine",),),
    6: (("near", 4, 0), ("across", 2), ("ready", 1, 1)),
    8: (("ready", 0, 3),),
    10: (("across", 3), ("ready", 1, 2)),
    12: (("ready", 0, 4), ("across", 4)),
    13: (("ready", 1, 3),),
    15: (("ready", 1, 4),),
}
SCALE = math.log2(math.e) / 16.0


def coarse_group(query, feat, first_block):
    rows = query.shape[0]
    sub = lax.broadcasted_iota(jnp.int32, (8, rows), 0)
    odd = (sub >= 4).astype(jnp.float32)
    top = jnp.full((8, rows), -jnp.inf, jnp.float32)
    total = jnp.zeros((8, rows), jnp.float32)
    row_sum = total
    col_sum = total
    for k in range(9):
        runs = 2 if k < 8 else 1
        size = 240 if k < 8 else 120
        scores = lax.dot_general(
            feat[k * 240 : k * 240 + size, :], query, NT, preferred_element_type=jnp.float32
        )
        scores = scores.reshape(runs * BLOCK, 8, rows)
        new_top = jnp.maximum(top, jnp.max(scores, axis=0))
        keep = jnp.exp2((top - new_top) * SCALE)
        top = new_top
        total = total * keep
        row_sum = row_sum * keep
        col_sum = col_sum * keep
        for h in range(runs):
            run = moment = None
            for a in range(BLOCK - 1, -1, -1):
                weight = jnp.exp2((scores[h * BLOCK + a] - top) * SCALE)
                run = weight if run is None else run + weight
                if a > 0:
                    moment = run if moment is None else moment + run
            block = first_block + (2 * k + h)
            row = (block // 4).astype(jnp.float32) - (GH - 1) / 2.0
            col = ((block % 4) * 30).astype(jnp.float32) - (GW - 1) / 2.0
            total = total + run
            row_sum = row_sum + run * row
            col_sum = col_sum + (run * (col + odd) + 2.0 * moment)
    both = jnp.maximum(top, pltpu.roll(top, 4, 0))
    keep = jnp.exp2((top - both) * SCALE)
    total = total * keep
    row_sum = row_sum * keep
    col_sum = col_sum * keep
    total = total + pltpu.roll(total, 4, 0)
    row_sum = row_sum + pltpu.roll(row_sum, 4, 0)
    col_sum = col_sum + pltpu.roll(col_sum, 4, 0)
    low = sub < 4
    return jnp.where(low, both, total), jnp.where(low, row_sum, col_sum)


def coarse_combine(stats, out):
    rows = stats.shape[-1]
    low = lax.broadcasted_iota(jnp.int32, (8, rows), 0) < 4
    tops = []
    for i in range(PEERS):
        first = stats[i, 0]
        tops.append(jnp.where(low, first, pltpu.roll(first, 4, 0)))
    top = functools.reduce(jnp.maximum, tops)
    total = jnp.zeros((8, rows), jnp.float32)
    sums = total
    for i in range(PEERS):
        factor = jnp.exp2((tops[i] - top) * SCALE)
        total = total + stats[i, 0] * factor
        sums = sums + stats[i, 1] * factor
    total = jnp.where(low, pltpu.roll(total, 4, 0), total)
    mean = sums / total
    head = lax.broadcasted_iota(jnp.int32, (rows, 128), 0) // 16
    track = lax.broadcasted_iota(jnp.int32, (rows, 128), 1)
    pick = (head == track).astype(jnp.float32)
    mean = jnp.dot(
        mean, pick, preferred_element_type=jnp.float32, precision=lax.Precision.HIGHEST
    ) * (1.0 / 16.0)
    low = lax.broadcasted_iota(jnp.int32, (8, 128), 0) < 4
    out[0:8, :] = mean * jnp.where(low, 1.0 / (GH / 4.0), 1.0 / (GW / 4.0))


def fine_frames(region, blk, frame_block, lists, valid, gathered, tiles, words, place, fscore, reply):
    lane = lax.broadcasted_iota(jnp.int32, (32, 128), 1)
    step = lax.broadcasted_iota(jnp.int32, (32, 128), 0)
    cell = blk * region + 2 * step + (lane >> 6)
    row = (cell * 34953) >> 22
    col = cell - row * GW
    place[0] = (row * TILE + ((lane & 63) >> 3)).astype(jnp.float32)
    place[1] = (col * TILE + (lane & 7)).astype(jnp.float32)
    words[...] = jnp.zeros_like(words)
    ids = lists[...]
    live = valid[...] > 0
    for k in range(4):
        bits = jnp.where(
            jnp.logical_and((ids >> 4) == k, live), jnp.left_shift(1, ids & 15), 0
        ).astype(jnp.float32)
        words[k * 4 : k * 4 + 4, 0:16] = jnp.sum(bits, axis=1)
    by_owner = jnp.transpose(words[...])[0:16]
    by_track = jnp.concatenate([by_owner, by_owner], axis=0)
    descs = jnp.concatenate([gathered[:, 0, :], gathered[:, 1, :]], axis=0).astype(jnp.bfloat16)
    track_row = jnp.concatenate([gathered[:, 2, :], gathered[:, 3, :]], axis=0)
    track_col = jnp.concatenate([gathered[:, 4, :], gathered[:, 5, :]], axis=0)
    right_half = lane >= 64

    def column(array, index):
        picked = jnp.sum(jnp.where(lane == index, array, 0.0), axis=1, keepdims=True)
        return jnp.broadcast_to(picked, (32, 128))

    def frame(w, results):
        at = frame_block * 4 + w
        here_row = column(track_row, at)
        here_col = column(track_col, at)
        masks = []
        for k in range(4):
            word = column(by_track, k * 4 + w).astype(jnp.int32)
            masks.append(jnp.where(right_half, word >> 1, word))
        top = jnp.full((32, 128), -1e30, jnp.float32)
        for q in range(8):
            scores = lax.dot_general(
                descs, tiles[w, q * 512 : q * 512 + 512, :], NT, preferred_element_type=jnp.float32
            ) * (1.0 / math.sqrt(128))
            for h in range(4):
                j = q * 4 + h
                away_row = place[0, j : j + 1, :] - here_row
                away_col = place[1, j : j + 1, :] - here_col
                score = scores[:, h * 128 : h * 128 + 128] - (
                    away_row * away_row + away_col * away_col
                ) * (0.5 / (SPREAD * SPREAD))
                listed = (masks[j // 8] & (1 << (2 * j % 16))) != 0
                score = jnp.where(listed, score, -1e30)
                fscore[j] = score
                top = jnp.maximum(top, score)
        top = jnp.broadcast_to(jnp.max(top, axis=1, keepdims=True), (32, 128))
        total = jnp.zeros((32, 128), jnp.float32)
        row_sum = total
        col_sum = total
        for j in range(32):
            weight = jnp.exp(fscore[j] - top)
            total = total + weight
            row_sum = row_sum + weight * (place[0, j : j + 1, :] - here_row)
            col_sum = col_sum + weight * (place[1, j : j + 1, :] - here_col)
        total = jnp.sum(total, axis=1, keepdims=True)
        row_out = jnp.sum(row_sum, axis=1, keepdims=True) / total * (1.0 / SPREAD)
        col_out = jnp.sum(col_sum, axis=1, keepdims=True) / total * (1.0 / SPREAD)
        here = lane == at
        return (
            jnp.where(here, row_out, results[0]),
            jnp.where(here, col_out, results[1]),
        )

    zeros = jnp.zeros((32, 128), jnp.float32)
    rows, cols = lax.fori_loop(0, 4, frame, (zeros, zeros))
    reply[...] = jnp.zeros_like(reply)
    reply[:, 0, :] = rows[0:16]
    reply[:, 1, :] = rows[16:32]
    reply[:, 2, :] = cols[0:16]
    reply[:, 3, :] = cols[16:32]


def kernel(
    q_in, feat, tiles_in, desc_in, pos_in, lists, valid,
    out,
    queries, tiles, stats_out, stats_in, gathered, reply, answers, words, place, fscore,
    local_sem, near_send, y_recv, z_recv, c_recv, far_send, far_recv, note_recv,
):
    blk = lax.axis_index("blk")
    frames = lax.axis_index("frames")
    z = blk & (RING - 1)
    yh = blk >> 3
    core = frames & 1
    half = pl.multiple_of(core * 256, 256)
    cross = {"blk": (1 - yh) * RING + z, "frames": frames + 2 - 2 * (frames & 2)}
    sibling = {"blk": blk, "frames": frames + 1 - 2 * core}

    def ring(k):
        return (z + (RING + k)) & (RING - 1)

    locals_ = [
        pltpu.make_async_copy(q_in, queries.at[z, yh], local_sem.at[0]),
        pltpu.make_async_copy(tiles_in, tiles, local_sem.at[1]),
    ]
    for c in locals_:
        c.start()

    barrier = pltpu.get_barrier_semaphore()

    def partner(bit):
        return {"blk": blk, "frames": frames + (1 << bit) - 2 * (frames & (1 << bit))}

    neighbours = [{"blk": yh * RING + ring(way), "frames": frames} for way in (1, -1)]
    for to in [cross, *neighbours, *(partner(bit) for bit in range(4))]:
        pl.semaphore_signal(barrier, inc=1, device_id=to)

    note = gathered.at[frames]
    note[...] = jnp.zeros((8, 128), jnp.float32)
    note[0:2, :] = desc_in[...].astype(jnp.float32)
    note[2:4, 0:64] = pos_in[0].astype(jnp.float32)
    note[4:6, 0:64] = pos_in[1].astype(jnp.float32)

    def remote(src, dst, send, recv, to):
        return pltpu.make_async_remote_copy(
            src_ref=src, dst_ref=dst, send_sem=send, recv_sem=recv,
            device_id=to, device_id_type=pl.DeviceIdType.MESH,
        )

    own = q_in.at[pl.ds(half, 256)]
    def part(chain, shift, start, size):
        return queries.at[ring(shift), yh if chain == 0 else 1 - yh, pl.ds(start, size)]

    def rows_of(chunk):
        return pl.multiple_of(half + 128 * chunk, 128)

    def z_copy(way, stage, chunk):
        to = {"blk": yh * RING + ring(1 - 2 * way), "frames": frames}
        at = 2 * (stage - 1) + chunk
        dst = part(0, (stage - 1) * (2 * way - 1), rows_of(chunk), 128)
        src = q_in.at[pl.ds(rows_of(chunk), 128)] if stage == 1 else dst
        return remote(src, dst, near_send.at[0], z_recv.at[way, at], to)

    def y_copy(way, stage, chunk):
        if stage == 0:
            return remote(own, part(0, 0, half, 256), near_send.at[1], y_recv.at[0, 8], cross)
        at = 2 * (stage - 1) + chunk
        ref = part(0, stage * (2 * way - 1), rows_of(chunk), 128)
        return remote(ref, ref, near_send.at[1], y_recv.at[way, at], cross)

    def c_copy(chain, way, stage):
        if stage == 0:
            k = 0
        elif stage < 4:
            k = 1 + chain * 6 + way * 3 + stage - 1
        else:
            k = 13 + chain
        ref = part(chain, stage * (2 * way - 1), half, 256)
        return remote(ref, ref, near_send.at[2], c_recv.at[k], sibling)

    Z_PARTS = [(w, d, c) for w in range(2) for d in range(1, 5) for c in range(2) if d < 4 or c == w]

    def note_copy(step):
        ref = gathered.at[pl.ds((frames >> step) << step, 1 << step)]
        return remote(ref, ref, far_send.at[0], note_recv.at[step], partner(step))

    def pass_note(step):
        note_copy(step - 1).wait_recv()
        note_copy(step).start()

    def answer_copy(i):
        to = (frames + i) & (PEERS - 1)
        return remote(
            reply.at[to], answers.at[i], far_send.at[1], far_recv.at[1], {"blk": blk, "frames": to}
        )

    def group_of(i):
        chain = away = i * 0
        for at, (n, k) in enumerate(ORDER):
            chain = jnp.where(i == at, n, chain)
            away = jnp.where(i == at, k, away)
        return (z + RING + away) & (RING - 1), (yh + chain) & 1

    def stat_copy(i):
        gz, gy = group_of(i)
        return remote(
            stats_out.at[i], stats_in.at[i], far_send.at[2], far_recv.at[2],
            {"blk": gy * RING + gz, "frames": frames},
        )

    def wait_all(ref, sem):
        pltpu.make_async_copy(ref, ref, sem).wait()

    def enter():
        pl.semaphore_wait(barrier, 7)
        for chunk in range(2):
            z_copy(0, 1, chunk).start()
            z_copy(1, 1, chunk).start()
        y_copy(0, 0, 0).start()
        note_copy(0).start()

    enter()
    locals_[0].wait()

    def fine_stage():
        locals_[1].wait()

        note_copy(3).wait_recv()
        fine_frames(
            510, blk, frames, lists, valid, gathered, tiles, words, place, fscore, reply
        )
        answers[0] = reply[frames]

        def start_answers(i, _):
            answer_copy(i).start()
            return 0

        lax.fori_loop(1, PEERS, start_answers, 0)

    def near(stage, chunk):
        for way in range(2):
            if stage == 4:
                chunk = way
            z_copy(way, stage, chunk).wait_recv()
            if stage < 3 or (stage == 3 and chunk == way):
                z_copy(way, stage + 1, chunk).start()
            y_copy(way, stage, chunk).start()
        if stage == 4:
            c_copy(0, 0, 4).start()
        elif chunk == 1:
            c_copy(0, 0, stage).start()
            c_copy(0, 1, stage).start()

    def across(stage):
        if stage == 0:
            y_copy(0, 0, 0).wait_recv()
            c_copy(1, 0, 0).start()
            return
        for way, d, chunk in Z_PARTS:
            if d == stage:
                y_copy(way, d, chunk).wait_recv()
        c_copy(1, 0, stage).start()
        if stage < 4:
            c_copy(1, 1, stage).start()

    def ready(chain, stage):
        c_copy(chain, 0, stage).wait_recv()
        if 0 < stage < 4:
            c_copy(chain, 1, stage).wait_recv()

    def group_step(i, _):
        for when, events in EVENTS.items():
            @pl.when(i == when)
            def _(events=events):
                for event, *at in events:
                    {"near": near, "across": across, "ready": ready, "fine": fine_stage, "note": pass_note}[event](*at)

        gz, gy = group_of(i)
        first, second = coarse_group(queries[gz, gy], feat, blk * 17)

        @pl.when(i == 0)
        def _():
            stats_in[0, 0] = first
            stats_in[0, 1] = second

        @pl.when(i > 0)
        def _():
            stats_out[i, 0] = first
            stats_out[i, 1] = second
            stat_copy(i).start()

        return 0

    lax.fori_loop(0, PEERS, group_step, 0)

    wait_all(answers.at[1:PEERS], far_recv.at[1])
    wait_all(stats_in.at[1:PEERS], far_recv.at[2])
    coarse_combine(stats_in, out)
    out[8:16, :] = jnp.sum(answers[...], axis=0)

    wait_all(gathered.at[1:PEERS], far_send.at[0])
    wait_all(answers.at[1:PEERS], far_send.at[1])
    wait_all(stats_in.at[1:PEERS], far_send.at[2])
    wait_all(queries.at[0:7, 0, 0:256], near_send.at[0])
    wait_all(queries.at[:, 0, 0:256], near_send.at[1])
    wait_all(queries.at[:, 0, 0:480], near_send.at[2])


def body(coarse_query, coarse_feat, fine_query, fine_tiles, track_pos, tile_list, tile_valid):
    track_group, heads, channels = coarse_query.shape
    frames_here, region, _ = coarse_feat.shape
    queries = coarse_query.reshape(track_group * heads, channels)
    feat = jnp.transpose(coarse_feat, (1, 0, 2)).reshape(region * frames_here, channels)
    tiles = fine_tiles.reshape(frames_here, -1, fine_tiles.shape[-1])
    pos = jnp.transpose(track_pos, (0, 2, 1))
    lists = jnp.transpose(tile_list[:, 0], (0, 2, 1))
    valid = jnp.transpose(tile_valid[:, 0], (0, 2, 1))
    f32 = jnp.float32
    vmem = pl.BlockSpec(memory_space=pltpu.VMEM)
    far = pl.BlockSpec(memory_space=pl.ANY)
    dma = pltpu.SemaphoreType.DMA
    rows = queries.shape[0]
    packed = pl.pallas_call(
        kernel,
        out_shape=jax.ShapeDtypeStruct((16, 128), f32),
        in_specs=[far, vmem, far, vmem, vmem, vmem, vmem],
        out_specs=vmem,
        scratch_shapes=[
            pltpu.VMEM((RING, 2, rows, channels), jnp.bfloat16),
            pltpu.VMEM(tiles.shape, jnp.bfloat16),
            pltpu.VMEM((PEERS, 2, 8, rows), f32),
            pltpu.VMEM((PEERS, 2, 8, rows), f32),
            pltpu.VMEM((PEERS, 8, 128), f32),
            pltpu.VMEM((PEERS, 8, 128), f32),
            pltpu.VMEM((PEERS, 8, 128), f32),
            pltpu.VMEM((128, 128), f32),
            pltpu.VMEM((2, 32, 128), f32),
            pltpu.VMEM((32, 32, 128), f32),
            dma((2,)),
            dma((3,)),
            dma((2, 9)),
            dma((2, 8)),
            dma((15,)),
            dma((3,)),
            dma((3,)),
            dma((4,)),
        ],
        compiler_params=pltpu.CompilerParams(
            collective_id=0, has_side_effects=True, vmem_limit_bytes=56 * 2**20
        ),
        cost_estimate=pl.CostEstimate(
            flops=2 * 8192 * 2048 * 256, bytes_accessed=6 * 10**6, transcendentals=8192 * 2048
        ),
    )(queries, feat, tiles, fine_query, pos, lists, valid)
    coarse_pos = packed[0:8, 0:32].reshape(2, 4, 32)
    offset = packed[8:12, 0:64].reshape(2, 2, 64)
    return coarse_pos, jnp.transpose(offset, (0, 2, 1))


def solution(mesh):
    return jax.shard_map(
        body,
        mesh=mesh,
        in_specs=(
            P("blk", None, None),
            P("frames", "blk", None),
            P(("blk", "frames"), None),
            P("frames", "blk", None, None),
            P(None, None, ("blk", "frames")),
            P("frames", "blk", None, None),
            P("frames", "blk", None, None),
        ),
        out_specs=(P(None, "frames", "blk"), P(None, None, ("blk", "frames"))),
        check_vma=False,
    )
```

```python
import functools
import math

import jax
import jax.numpy as jnp
from jax import lax
from jax.experimental import pallas as pl
from jax.experimental.pallas import tpu as pltpu
from jax.sharding import PartitionSpec as P

GH = 68
GW = 120
TILE = 8
SPREAD = 32.0
NT = (((1,), (1,)), ((), ()))
RING = 8
PEERS = 16
BLOCK = 15
ORDER = (
    (0, 0), (1, 0), (0, -1), (0, 1), (0, -2), (0, 2), (1, -1), (1, 1),
    (0, -3), (0, 3), (1, -2), (1, 2), (0, 4), (1, -3), (1, 3), (1, 4),
)
EVENTS = {
    1: (
        ("near", 1, 0), ("near", 1, 1), ("across", 0), ("fine",), ("near", 2, 0), ("near", 2, 1), ("ready", 1, 0),
    ),
    2: (("ready", 0, 1),),
    3: (("near", 3, 0),),
    4: (("near", 3, 1), ("across", 1), ("ready", 0, 2)),
    6: (("ready", 1, 1),),
    7: (("near", 4, 0), ("across", 2)),
    8: (("ready", 0, 3),),
    10: (("across", 3), ("ready", 1, 2)),
    12: (("ready", 0, 4), ("across", 4)),
    13: (("ready", 1, 3),),
    15: (("ready", 1, 4),),
}
SCALE = math.log2(math.e) / 16.0


def coarse_group(query, feat, first_block):
    rows = query.shape[0]
    sub = lax.broadcasted_iota(jnp.int32, (8, rows), 0)
    odd = (sub >= 4).astype(jnp.float32)
    top = jnp.full((8, rows), -jnp.inf, jnp.float32)
    total = jnp.zeros((8, rows), jnp.float32)
    row_sum = total
    col_sum = total
    for k in range(9):
        runs = 2 if k < 8 else 1
        size = 240 if k < 8 else 120
        scores = lax.dot_general(
            feat[k * 240 : k * 240 + size, :], query, NT, preferred_element_type=jnp.float32
        )
        scores = scores.reshape(runs * BLOCK, 8, rows)
        new_top = jnp.maximum(top, jnp.max(scores, axis=0))
        keep = jnp.exp2((top - new_top) * SCALE)
        top = new_top
        total = total * keep
        row_sum = row_sum * keep
        col_sum = col_sum * keep
        for h in range(runs):
            run = moment = None
            for a in range(BLOCK - 1, -1, -1):
                weight = jnp.exp2((scores[h * BLOCK + a] - top) * SCALE)
                run = weight if run is None else run + weight
                if a > 0:
                    moment = run if moment is None else moment + run
            block = first_block + (2 * k + h)
            row = (block // 4).astype(jnp.float32) - (GH - 1) / 2.0
            col = ((block % 4) * 30).astype(jnp.float32) - (GW - 1) / 2.0
            total = total + run
            row_sum = row_sum + run * row
            col_sum = col_sum + (run * (col + odd) + 2.0 * moment)
    both = jnp.maximum(top, pltpu.roll(top, 4, 0))
    keep = jnp.exp2((top - both) * SCALE)
    total = total * keep
    row_sum = row_sum * keep
    col_sum = col_sum * keep
    total = total + pltpu.roll(total, 4, 0)
    row_sum = row_sum + pltpu.roll(row_sum, 4, 0)
    col_sum = col_sum + pltpu.roll(col_sum, 4, 0)
    low = sub < 4
    return jnp.where(low, both, total), jnp.where(low, row_sum, col_sum)


def coarse_combine(stats, out):
    rows = stats.shape[-1]
    low = lax.broadcasted_iota(jnp.int32, (8, rows), 0) < 4
    tops = []
    for i in range(PEERS):
        first = stats[i, 0]
        tops.append(jnp.where(low, first, pltpu.roll(first, 4, 0)))
    top = functools.reduce(jnp.maximum, tops)
    total = jnp.zeros((8, rows), jnp.float32)
    sums = total
    for i in range(PEERS):
        factor = jnp.exp2((tops[i] - top) * SCALE)
        total = total + stats[i, 0] * factor
        sums = sums + stats[i, 1] * factor
    total = jnp.where(low, pltpu.roll(total, 4, 0), total)
    mean = sums / total
    head = lax.broadcasted_iota(jnp.int32, (rows, 128), 0) // 16
    track = lax.broadcasted_iota(jnp.int32, (rows, 128), 1)
    pick = (head == track).astype(jnp.float32)
    mean = jnp.dot(
        mean, pick, preferred_element_type=jnp.float32, precision=lax.Precision.HIGHEST
    ) * (1.0 / 16.0)
    low = lax.broadcasted_iota(jnp.int32, (8, 128), 0) < 4
    out[0:8, :] = mean * jnp.where(low, 1.0 / (GH / 4.0), 1.0 / (GW / 4.0))


def fine_frames(region, blk, frame_block, lists, valid, gathered, tiles, words, place, fscore, reply):
    lane = lax.broadcasted_iota(jnp.int32, (32, 128), 1)
    step = lax.broadcasted_iota(jnp.int32, (32, 128), 0)
    cell = blk * region + 2 * step + (lane >> 6)
    row = (cell * 34953) >> 22
    col = cell - row * GW
    place[0] = (row * TILE + ((lane & 63) >> 3)).astype(jnp.float32)
    place[1] = (col * TILE + (lane & 7)).astype(jnp.float32)
    words[...] = jnp.zeros_like(words)
    ids = lists[...]
    live = valid[...] > 0
    for k in range(4):
        bits = jnp.where(
            jnp.logical_and((ids >> 4) == k, live), jnp.left_shift(1, ids & 15), 0
        ).astype(jnp.float32)
        words[k * 4 : k * 4 + 4, 0:16] = jnp.sum(bits, axis=1)
    by_owner = jnp.transpose(words[...])[0:16]
    by_track = jnp.concatenate([by_owner, by_owner], axis=0)
    descs = jnp.concatenate([gathered[:, 0, :], gathered[:, 1, :]], axis=0).astype(jnp.bfloat16)
    track_row = jnp.concatenate([gathered[:, 2, :], gathered[:, 3, :]], axis=0)
    track_col = jnp.concatenate([gathered[:, 4, :], gathered[:, 5, :]], axis=0)
    right_half = lane >= 64

    def column(array, index):
        picked = jnp.sum(jnp.where(lane == index, array, 0.0), axis=1, keepdims=True)
        return jnp.broadcast_to(picked, (32, 128))

    def frame(w, results):
        at = frame_block * 4 + w
        here_row = column(track_row, at)
        here_col = column(track_col, at)
        masks = []
        for k in range(4):
            word = column(by_track, k * 4 + w).astype(jnp.int32)
            masks.append(jnp.where(right_half, word >> 1, word))
        top = jnp.full((32, 128), -1e30, jnp.float32)
        for q in range(8):
            scores = lax.dot_general(
                descs, tiles[w, q * 512 : q * 512 + 512, :], NT, preferred_element_type=jnp.float32
            ) * (1.0 / math.sqrt(128))
            for h in range(4):
                j = q * 4 + h
                away_row = place[0, j : j + 1, :] - here_row
                away_col = place[1, j : j + 1, :] - here_col
                score = scores[:, h * 128 : h * 128 + 128] - (
                    away_row * away_row + away_col * away_col
                ) * (0.5 / (SPREAD * SPREAD))
                listed = (masks[j // 8] & (1 << (2 * j % 16))) != 0
                score = jnp.where(listed, score, -1e30)
                fscore[j] = score
                top = jnp.maximum(top, score)
        top = jnp.broadcast_to(jnp.max(top, axis=1, keepdims=True), (32, 128))
        total = jnp.zeros((32, 128), jnp.float32)
        row_sum = total
        col_sum = total
        for j in range(32):
            weight = jnp.exp(fscore[j] - top)
            total = total + weight
            row_sum = row_sum + weight * (place[0, j : j + 1, :] - here_row)
            col_sum = col_sum + weight * (place[1, j : j + 1, :] - here_col)
        total = jnp.sum(total, axis=1, keepdims=True)
        row_out = jnp.sum(row_sum, axis=1, keepdims=True) / total * (1.0 / SPREAD)
        col_out = jnp.sum(col_sum, axis=1, keepdims=True) / total * (1.0 / SPREAD)
        here = lane == at
        return (
            jnp.where(here, row_out, results[0]),
            jnp.where(here, col_out, results[1]),
        )

    zeros = jnp.zeros((32, 128), jnp.float32)
    rows, cols = lax.fori_loop(0, 4, frame, (zeros, zeros))
    reply[...] = jnp.zeros_like(reply)
    reply[:, 0, :] = rows[0:16]
    reply[:, 1, :] = rows[16:32]
    reply[:, 2, :] = cols[0:16]
    reply[:, 3, :] = cols[16:32]


def kernel(
    q_in, f_in, tiles_in, desc_in, pos_in, lists, valid,
    out,
    queries, raw, feat, tiles, stats_out, stats_in, gathered, reply, answers, words, place, fscore,
    local_sem, near_send, y_recv, z_recv, c_recv, far_send, far_recv,
):
    blk = lax.axis_index("blk")
    frames = lax.axis_index("frames")
    z = blk & (RING - 1)
    yh = blk >> 3
    core = frames & 1
    half = pl.multiple_of(core * 256, 256)
    cross = {"blk": (1 - yh) * RING + z, "frames": frames + 2 - 2 * (frames & 2)}
    sibling = {"blk": blk, "frames": frames + 1 - 2 * core}

    def ring(k):
        return (z + (RING + k)) & (RING - 1)

    locals_ = [
        pltpu.make_async_copy(q_in, queries.at[z, yh], local_sem.at[0]),
        pltpu.make_async_copy(tiles_in, tiles, local_sem.at[1]),
        pltpu.make_async_copy(f_in, raw, local_sem.at[2]),
    ]
    for c in locals_:
        c.start()

    barrier = pltpu.get_barrier_semaphore()

    def greet(i, _):
        pl.semaphore_signal(barrier, inc=1, device_id={"blk": (blk + i) & (PEERS - 1), "frames": frames})
        pl.semaphore_signal(barrier, inc=1, device_id={"blk": blk, "frames": (frames + i) & (PEERS - 1)})
        return 0

    lax.fori_loop(1, PEERS, greet, 0)
    pl.semaphore_signal(barrier, inc=1, device_id=cross)

    note = gathered.at[frames]
    note[...] = jnp.zeros((8, 128), jnp.float32)
    note[0:2, :] = desc_in[...].astype(jnp.float32)
    note[2:4, 0:64] = pos_in[0].astype(jnp.float32)
    note[4:6, 0:64] = pos_in[1].astype(jnp.float32)

    def remote(src, dst, send, recv, to):
        return pltpu.make_async_remote_copy(
            src_ref=src, dst_ref=dst, send_sem=send, recv_sem=recv,
            device_id=to, device_id_type=pl.DeviceIdType.MESH,
        )

    own = q_in.at[pl.ds(half, 256)]
    def part(chain, shift, start, size):
        return queries.at[ring(shift), yh if chain == 0 else 1 - yh, pl.ds(start, size)]

    def rows_of(chunk):
        return pl.multiple_of(half + 128 * chunk, 128)

    def z_copy(way, stage, chunk):
        to = {"blk": yh * RING + ring(1 - 2 * way), "frames": frames}
        at = 2 * (stage - 1) + chunk
        dst = part(0, (stage - 1) * (2 * way - 1), rows_of(chunk), 128)
        src = q_in.at[pl.ds(rows_of(chunk), 128)] if stage == 1 else dst
        return remote(src, dst, near_send.at[0], z_recv.at[way, at], to)

    def y_copy(way, stage, chunk):
        if stage == 0:
            return remote(own, part(0, 0, half, 256), near_send.at[1], y_recv.at[0, 8], cross)
        at = 2 * (stage - 1) + chunk
        ref = part(0, stage * (2 * way - 1), rows_of(chunk), 128)
        return remote(ref, ref, near_send.at[1], y_recv.at[way, at], cross)

    def c_copy(chain, way, stage):
        if stage == 0:
            k = 0
        elif stage < 4:
            k = 1 + chain * 6 + way * 3 + stage - 1
        else:
            k = 13 + chain
        ref = part(chain, stage * (2 * way - 1), half, 256)
        return remote(ref, ref, near_send.at[2], c_recv.at[k], sibling)

    Z_PARTS = [(w, d, c) for w in range(2) for d in range(1, 5) for c in range(2) if d < 4 or c == w]

    def note_copy(i):
        return remote(
            note, note, far_send.at[0], far_recv.at[0],
            {"blk": blk, "frames": (frames + i) & (PEERS - 1)},
        )

    def answer_copy(i):
        to = (frames + i) & (PEERS - 1)
        return remote(
            reply.at[to], answers.at[i], far_send.at[1], far_recv.at[1], {"blk": blk, "frames": to}
        )

    def group_of(i):
        chain = away = i * 0
        for at, (n, k) in enumerate(ORDER):
            chain = jnp.where(i == at, n, chain)
            away = jnp.where(i == at, k, away)
        return (z + RING + away) & (RING - 1), (yh + chain) & 1

    def stat_copy(i):
        gz, gy = group_of(i)
        return remote(
            stats_out.at[i], stats_in.at[i], far_send.at[2], far_recv.at[2],
            {"blk": gy * RING + gz, "frames": frames},
        )

    def wait_all(ref, sem):
        pltpu.make_async_copy(ref, ref, sem).wait()

    def start_notes(i, _):
        note_copy(i).start()
        return 0

    def enter():
        pl.semaphore_wait(barrier, 2 * (PEERS - 1) + 1)
        for chunk in range(2):
            z_copy(0, 1, chunk).start()
            z_copy(1, 1, chunk).start()
        y_copy(0, 0, 0).start()
        lax.fori_loop(1, PEERS, start_notes, 0)

    enter()
    locals_[2].wait()
    for cells in range(0, 510, 60):
        size = min(60, 510 - cells)
        feat[cells * 4 : (cells + size) * 4, :] = raw[cells : cells + size].reshape(size * 4, 256)
    locals_[0].wait()

    def fine_stage():
        locals_[1].wait()

        wait_all(gathered.at[1:PEERS], far_recv.at[0])
        fine_frames(
            510, blk, frames, lists, valid, gathered, tiles, words, place, fscore, reply
        )
        answers[0] = reply[frames]

        def start_answers(i, _):
            answer_copy(i).start()
            return 0

        lax.fori_loop(1, PEERS, start_answers, 0)

    def near(stage, chunk):
        for way in range(2):
            if stage == 4:
                chunk = way
            z_copy(way, stage, chunk).wait_recv()
            if stage < 3 or (stage == 3 and chunk == way):
                z_copy(way, stage + 1, chunk).start()
            y_copy(way, stage, chunk).start()
        if stage == 4:
            c_copy(0, 0, 4).start()
        elif chunk == 1:
            c_copy(0, 0, stage).start()
            c_copy(0, 1, stage).start()

    def across(stage):
        if stage == 0:
            y_copy(0, 0, 0).wait_recv()
            c_copy(1, 0, 0).start()
            return
        for way, d, chunk in Z_PARTS:
            if d == stage:
                y_copy(way, d, chunk).wait_recv()
        c_copy(1, 0, stage).start()
        if stage < 4:
            c_copy(1, 1, stage).start()

    def ready(chain, stage):
        c_copy(chain, 0, stage).wait_recv()
        if 0 < stage < 4:
            c_copy(chain, 1, stage).wait_recv()

    def group_step(i, _):
        for when, events in EVENTS.items():
            @pl.when(i == when)
            def _(events=events):
                for event, *at in events:
                    {"near": near, "across": across, "ready": ready, "fine": fine_stage}[event](*at)

        gz, gy = group_of(i)
        first, second = coarse_group(queries[gz, gy], feat, blk * 17)

        @pl.when(i == 0)
        def _():
            stats_in[0, 0] = first
            stats_in[0, 1] = second

        @pl.when(i > 0)
        def _():
            stats_out[i, 0] = first
            stats_out[i, 1] = second
            stat_copy(i).start()

        return 0

    lax.fori_loop(0, PEERS, group_step, 0)

    wait_all(answers.at[1:PEERS], far_recv.at[1])
    wait_all(stats_in.at[1:PEERS], far_recv.at[2])
    coarse_combine(stats_in, out)
    out[8:16, :] = jnp.sum(answers[...], axis=0)

    wait_all(gathered.at[1:PEERS], far_send.at[0])
    wait_all(answers.at[1:PEERS], far_send.at[1])
    wait_all(stats_in.at[1:PEERS], far_send.at[2])
    wait_all(queries.at[0:7, 0, 0:256], near_send.at[0])
    wait_all(queries.at[:, 0, 0:256], near_send.at[1])
    wait_all(queries.at[:, 0, 0:480], near_send.at[2])


def split_result(packed, coarse_pos, offset):
    for i in range(2):
        coarse_pos[i] = packed[4 * i : 4 * i + 4, 0:32]
        offset[i] = packed[8 + 2 * i : 10 + 2 * i, 0:64]


def body(coarse_query, coarse_feat, fine_query, fine_tiles, track_pos, tile_list, tile_valid):
    track_group, heads, channels = coarse_query.shape
    frames_here, region, _ = coarse_feat.shape
    queries = coarse_query.reshape(track_group * heads, channels)
    feat = jnp.transpose(coarse_feat, (1, 0, 2))
    tiles = fine_tiles.reshape(frames_here, -1, fine_tiles.shape[-1])
    pos = jnp.transpose(track_pos, (0, 2, 1))
    lists = jnp.transpose(tile_list[:, 0], (0, 2, 1))
    valid = jnp.transpose(tile_valid[:, 0], (0, 2, 1))
    f32 = jnp.float32
    vmem = pl.BlockSpec(memory_space=pltpu.VMEM)
    far = pl.BlockSpec(memory_space=pl.ANY)
    dma = pltpu.SemaphoreType.DMA
    rows = queries.shape[0]
    packed = pl.pallas_call(
        kernel,
        out_shape=jax.ShapeDtypeStruct((16, 128), f32),
        in_specs=[far, far, far, vmem, vmem, vmem, vmem],
        out_specs=vmem,
        scratch_shapes=[
            pltpu.VMEM((RING, 2, rows, channels), jnp.bfloat16),
            pltpu.VMEM(feat.shape, jnp.bfloat16),
            pltpu.VMEM((region * frames_here, channels), jnp.bfloat16),
            pltpu.VMEM(tiles.shape, jnp.bfloat16),
            pltpu.VMEM((PEERS, 2, 8, rows), f32),
            pltpu.VMEM((PEERS, 2, 8, rows), f32),
            pltpu.VMEM((PEERS, 8, 128), f32),
            pltpu.VMEM((PEERS, 8, 128), f32),
            pltpu.VMEM((PEERS, 8, 128), f32),
            pltpu.VMEM((128, 128), f32),
            pltpu.VMEM((2, 32, 128), f32),
            pltpu.VMEM((32, 32, 128), f32),
            dma((3,)),
            dma((3,)),
            dma((2, 9)),
            dma((2, 8)),
            dma((15,)),
            dma((3,)),
            dma((3,)),
        ],
        compiler_params=pltpu.CompilerParams(
            collective_id=0, has_side_effects=True, vmem_limit_bytes=56 * 2**20
        ),
        cost_estimate=pl.CostEstimate(
            flops=2 * 8192 * 2048 * 256, bytes_accessed=6 * 10**6, transcendentals=8192 * 2048
        ),
    )(queries, feat, tiles, fine_query, pos, lists, valid)
    coarse_pos, offset = pl.pallas_call(
        split_result,
        out_shape=(
            jax.ShapeDtypeStruct((2, 4, 32), f32),
            jax.ShapeDtypeStruct((2, 2, 64), f32),
        ),
        in_specs=[vmem],
        out_specs=(vmem, vmem),
    )(packed)
    return coarse_pos, jnp.transpose(offset, (0, 2, 1))


def solution(mesh):
    return jax.shard_map(
        body,
        mesh=mesh,
        in_specs=(
            P("blk", None, None),
            P("frames", "blk", None),
            P(("blk", "frames"), None),
            P("frames", "blk", None, None),
            P(None, None, ("blk", "frames")),
            P("frames", "blk", None, None),
            P("frames", "blk", None, None),
        ),
        out_specs=(P(None, "frames", "blk"), P(None, None, ("blk", "frames"))),
        check_vma=False,
    )
```

```python
import functools
import math

import jax
import jax.numpy as jnp
from jax import lax
from jax.experimental import pallas as pl
from jax.experimental.pallas import tpu as pltpu
from jax.sharding import PartitionSpec as P

GH = 68
GW = 120
TILE = 8
SPREAD = 32.0
NT = (((1,), (1,)), ((), ()))
RING = 8
PEERS = 16
BLOCK = 15
ORDER = (
    (0, 0), (1, 0), (0, -1), (0, 1), (0, -2), (0, 2), (1, -1), (1, 1),
    (0, -3), (0, 3), (1, -2), (1, 2), (0, 4), (1, -3), (1, 3), (1, 4),
)
EVENTS = {
    1: (
        ("near", 1, 0), ("near", 1, 1), ("across", 0), ("fine",), ("near", 2, 0), ("near", 2, 1), ("ready", 1, 0),
    ),
    2: (("ready", 0, 1),),
    3: (("near", 3, 0),),
    4: (("near", 3, 1), ("across", 1), ("ready", 0, 2)),
    6: (("ready", 1, 1),),
    7: (("near", 4, 0), ("across", 2)),
    8: (("ready", 0, 3),),
    10: (("ready", 1, 2),),
    11: (("across", 3),),
    12: (("ready", 0, 4),),
    13: (("across", 4), ("ready", 1, 3)),
    15: (("ready", 1, 4),),
}
SCALE = math.log2(math.e) / 16.0


def coarse_group(query, feat, first_block):
    rows = query.shape[0]
    sub = lax.broadcasted_iota(jnp.int32, (8, rows), 0)
    odd = (sub >= 4).astype(jnp.float32)
    top = jnp.full((8, rows), -jnp.inf, jnp.float32)
    total = jnp.zeros((8, rows), jnp.float32)
    row_sum = total
    col_sum = total
    for k in range(9):
        runs = 2 if k < 8 else 1
        size = 240 if k < 8 else 120
        scores = lax.dot_general(
            feat[k * 240 : k * 240 + size, :], query, NT, preferred_element_type=jnp.float32
        )
        scores = scores.reshape(runs * BLOCK, 8, rows)
        new_top = jnp.maximum(top, jnp.max(scores, axis=0))
        keep = jnp.exp2((top - new_top) * SCALE)
        top = new_top
        total = total * keep
        row_sum = row_sum * keep
        col_sum = col_sum * keep
        for h in range(runs):
            run = moment = None
            for a in range(BLOCK - 1, -1, -1):
                weight = jnp.exp2((scores[h * BLOCK + a] - top) * SCALE)
                run = weight if run is None else run + weight
                if a > 0:
                    moment = run if moment is None else moment + run
            block = first_block + (2 * k + h)
            row = (block // 4).astype(jnp.float32) - (GH - 1) / 2.0
            col = ((block % 4) * 30).astype(jnp.float32) - (GW - 1) / 2.0
            total = total + run
            row_sum = row_sum + run * row
            col_sum = col_sum + (run * (col + odd) + 2.0 * moment)
    both = jnp.maximum(top, pltpu.roll(top, 4, 0))
    keep = jnp.exp2((top - both) * SCALE)
    total = total * keep
    row_sum = row_sum * keep
    col_sum = col_sum * keep
    total = total + pltpu.roll(total, 4, 0)
    row_sum = row_sum + pltpu.roll(row_sum, 4, 0)
    col_sum = col_sum + pltpu.roll(col_sum, 4, 0)
    low = sub < 4
    return jnp.where(low, both, total), jnp.where(low, row_sum, col_sum)


def coarse_combine(stats, out):
    rows = stats.shape[-1]
    low = lax.broadcasted_iota(jnp.int32, (8, rows), 0) < 4
    tops = []
    for i in range(PEERS):
        first = stats[i, 0]
        tops.append(jnp.where(low, first, pltpu.roll(first, 4, 0)))
    top = functools.reduce(jnp.maximum, tops)
    total = jnp.zeros((8, rows), jnp.float32)
    sums = total
    for i in range(PEERS):
        factor = jnp.exp2((tops[i] - top) * SCALE)
        total = total + stats[i, 0] * factor
        sums = sums + stats[i, 1] * factor
    total = jnp.where(low, pltpu.roll(total, 4, 0), total)
    mean = sums / total
    head = lax.broadcasted_iota(jnp.int32, (rows, 128), 0) // 16
    track = lax.broadcasted_iota(jnp.int32, (rows, 128), 1)
    pick = (head == track).astype(jnp.float32)
    mean = jnp.dot(
        mean, pick, preferred_element_type=jnp.float32, precision=lax.Precision.HIGHEST
    ) * (1.0 / 16.0)
    low = lax.broadcasted_iota(jnp.int32, (8, 128), 0) < 4
    out[0:8, :] = mean * jnp.where(low, 1.0 / (GH / 4.0), 1.0 / (GW / 4.0))


def fine_frames(region, blk, frame_block, lists, valid, gathered, tiles, words, place, fscore, reply):
    lane = lax.broadcasted_iota(jnp.int32, (32, 128), 1)
    step = lax.broadcasted_iota(jnp.int32, (32, 128), 0)
    cell = blk * region + 2 * step + (lane >> 6)
    row = (cell * 34953) >> 22
    col = cell - row * GW
    place[0] = (row * TILE + ((lane & 63) >> 3)).astype(jnp.float32)
    place[1] = (col * TILE + (lane & 7)).astype(jnp.float32)
    words[...] = jnp.zeros_like(words)
    ids = lists[...]
    live = valid[...] > 0
    for k in range(4):
        bits = jnp.where(
            jnp.logical_and((ids >> 4) == k, live), jnp.left_shift(1, ids & 15), 0
        ).astype(jnp.float32)
        words[k * 4 : k * 4 + 4, 0:16] = jnp.sum(bits, axis=1)
    by_owner = jnp.transpose(words[...])[0:16]
    by_track = jnp.concatenate([by_owner, by_owner], axis=0)
    descs = jnp.concatenate([gathered[:, 0, :], gathered[:, 1, :]], axis=0).astype(jnp.bfloat16)
    track_row = jnp.concatenate([gathered[:, 2, :], gathered[:, 3, :]], axis=0)
    track_col = jnp.concatenate([gathered[:, 4, :], gathered[:, 5, :]], axis=0)
    right_half = lane >= 64

    def column(array, index):
        picked = jnp.sum(jnp.where(lane == index, array, 0.0), axis=1, keepdims=True)
        return jnp.broadcast_to(picked, (32, 128))

    def frame(w, results):
        at = frame_block * 4 + w
        here_row = column(track_row, at)
        here_col = column(track_col, at)
        masks = []
        for k in range(4):
            word = column(by_track, k * 4 + w).astype(jnp.int32)
            masks.append(jnp.where(right_half, word >> 1, word))
        top = jnp.full((32, 128), -1e30, jnp.float32)
        for q in range(8):
            scores = lax.dot_general(
                descs, tiles[w, q * 512 : q * 512 + 512, :], NT, preferred_element_type=jnp.float32
            ) * (1.0 / math.sqrt(128))
            for h in range(4):
                j = q * 4 + h
                away_row = place[0, j : j + 1, :] - here_row
                away_col = place[1, j : j + 1, :] - here_col
                score = scores[:, h * 128 : h * 128 + 128] - (
                    away_row * away_row + away_col * away_col
                ) * (0.5 / (SPREAD * SPREAD))
                listed = (masks[j // 8] & (1 << (2 * j % 16))) != 0
                score = jnp.where(listed, score, -1e30)
                fscore[j] = score
                top = jnp.maximum(top, score)
        top = jnp.broadcast_to(jnp.max(top, axis=1, keepdims=True), (32, 128))
        total = jnp.zeros((32, 128), jnp.float32)
        row_sum = total
        col_sum = total
        for j in range(32):
            weight = jnp.exp(fscore[j] - top)
            total = total + weight
            row_sum = row_sum + weight * (place[0, j : j + 1, :] - here_row)
            col_sum = col_sum + weight * (place[1, j : j + 1, :] - here_col)
        total = jnp.sum(total, axis=1, keepdims=True)
        row_out = jnp.sum(row_sum, axis=1, keepdims=True) / total * (1.0 / SPREAD)
        col_out = jnp.sum(col_sum, axis=1, keepdims=True) / total * (1.0 / SPREAD)
        here = lane == at
        return (
            jnp.where(here, row_out, results[0]),
            jnp.where(here, col_out, results[1]),
        )

    zeros = jnp.zeros((32, 128), jnp.float32)
    rows, cols = lax.fori_loop(0, 4, frame, (zeros, zeros))
    reply[...] = jnp.zeros_like(reply)
    reply[:, 0, :] = rows[0:16]
    reply[:, 1, :] = rows[16:32]
    reply[:, 2, :] = cols[0:16]
    reply[:, 3, :] = cols[16:32]


def kernel(
    q_in, f_in, tiles_in, desc_in, pos_in, lists, valid,
    out,
    queries, raw, feat, tiles, stats_out, stats_in, gathered, reply, answers, words, place, fscore,
    local_sem, near_send, y_recv, z_recv, c_recv, far_send, far_recv,
):
    blk = lax.axis_index("blk")
    frames = lax.axis_index("frames")
    z = blk & (RING - 1)
    yh = blk >> 3
    core = frames & 1
    half = pl.multiple_of(core * 256, 256)
    cross = {"blk": (1 - yh) * RING + z, "frames": frames + 2 - 2 * (frames & 2)}
    sibling = {"blk": blk, "frames": frames + 1 - 2 * core}

    def ring(k):
        return (z + (RING + k)) & (RING - 1)

    locals_ = [
        pltpu.make_async_copy(q_in, queries.at[z, yh], local_sem.at[0]),
        pltpu.make_async_copy(tiles_in, tiles, local_sem.at[1]),
        pltpu.make_async_copy(f_in, raw, local_sem.at[2]),
    ]
    for c in locals_:
        c.start()

    barrier = pltpu.get_barrier_semaphore()

    def greet(i, _):
        pl.semaphore_signal(barrier, inc=1, device_id={"blk": (blk + i) & (PEERS - 1), "frames": frames})
        pl.semaphore_signal(barrier, inc=1, device_id={"blk": blk, "frames": (frames + i) & (PEERS - 1)})
        return 0

    lax.fori_loop(1, PEERS, greet, 0)
    pl.semaphore_signal(barrier, inc=1, device_id=cross)

    note = gathered.at[frames]
    note[...] = jnp.zeros((8, 128), jnp.float32)
    note[0:2, :] = desc_in[...].astype(jnp.float32)
    note[2:4, 0:64] = pos_in[0].astype(jnp.float32)
    note[4:6, 0:64] = pos_in[1].astype(jnp.float32)

    def remote(src, dst, send, recv, to):
        return pltpu.make_async_remote_copy(
            src_ref=src, dst_ref=dst, send_sem=send, recv_sem=recv,
            device_id=to, device_id_type=pl.DeviceIdType.MESH,
        )

    own = q_in.at[pl.ds(half, 256)]
    def part(chain, shift, start, size):
        return queries.at[ring(shift), yh if chain == 0 else 1 - yh, pl.ds(start, size)]

    def rows_of(chunk):
        return pl.multiple_of(half + 128 * chunk, 128)

    def z_copy(way, stage, chunk):
        to = {"blk": yh * RING + ring(1 - 2 * way), "frames": frames}
        at = 2 * (stage - 1) + chunk
        dst = part(0, (stage - 1) * (2 * way - 1), rows_of(chunk), 128)
        src = q_in.at[pl.ds(rows_of(chunk), 128)] if stage == 1 else dst
        return remote(src, dst, near_send.at[0], z_recv.at[way, at], to)

    def y_copy(way, stage, chunk):
        if stage == 0:
            return remote(own, part(0, 0, half, 256), near_send.at[1], y_recv.at[0, 8], cross)
        at = 2 * (stage - 1) + chunk
        ref = part(0, stage * (2 * way - 1), rows_of(chunk), 128)
        return remote(ref, ref, near_send.at[1], y_recv.at[way, at], cross)

    def c_copy(chain, way, stage):
        if stage == 0:
            k = 0
        elif stage < 4:
            k = 1 + chain * 6 + way * 3 + stage - 1
        else:
            k = 13 + chain
        ref = part(chain, stage * (2 * way - 1), half, 256)
        return remote(ref, ref, near_send.at[2], c_recv.at[k], sibling)

    Z_PARTS = [(w, d, c) for w in range(2) for d in range(1, 5) for c in range(2) if d < 4 or c == w]

    def note_copy(i):
        return remote(
            note, note, far_send.at[0], far_recv.at[0],
            {"blk": blk, "frames": (frames + i) & (PEERS - 1)},
        )

    def answer_copy(i):
        to = (frames + i) & (PEERS - 1)
        return remote(
            reply.at[to], answers.at[i], far_send.at[1], far_recv.at[1], {"blk": blk, "frames": to}
        )

    def group_of(i):
        chain = away = i * 0
        for at, (n, k) in enumerate(ORDER):
            chain = jnp.where(i == at, n, chain)
            away = jnp.where(i == at, k, away)
        return (z + RING + away) & (RING - 1), (yh + chain) & 1

    def stat_copy(i):
        gz, gy = group_of(i)
        return remote(
            stats_out.at[i], stats_in.at[i], far_send.at[2], far_recv.at[2],
            {"blk": gy * RING + gz, "frames": frames},
        )

    def wait_all(ref, sem):
        pltpu.make_async_copy(ref, ref, sem).wait()

    def start_notes(i, _):
        note_copy(i).start()
        return 0

    def enter():
        pl.semaphore_wait(barrier, 2 * (PEERS - 1) + 1)
        for chunk in range(2):
            z_copy(0, 1, chunk).start()
            z_copy(1, 1, chunk).start()
        y_copy(0, 0, 0).start()
        lax.fori_loop(1, PEERS, start_notes, 0)

    enter()
    locals_[2].wait()
    for cells in range(0, 510, 60):
        size = min(60, 510 - cells)
        feat[cells * 4 : (cells + size) * 4, :] = raw[cells : cells + size].reshape(size * 4, 256)
    locals_[0].wait()

    def fine_stage():
        locals_[1].wait()

        wait_all(gathered.at[1:PEERS], far_recv.at[0])
        fine_frames(
            510, blk, frames, lists, valid, gathered, tiles, words, place, fscore, reply
        )
        answers[0] = reply[frames]

        def start_answers(i, _):
            answer_copy(i).start()
            return 0

        lax.fori_loop(1, PEERS, start_answers, 0)

    def near(stage, chunk):
        for way in range(2):
            if stage == 4:
                chunk = way
            z_copy(way, stage, chunk).wait_recv()
            if stage < 3 or (stage == 3 and chunk == way):
                z_copy(way, stage + 1, chunk).start()
            y_copy(way, stage, chunk).start()
        if stage == 4:
            c_copy(0, 0, 4).start()
        elif chunk == 1:
            c_copy(0, 0, stage).start()
            c_copy(0, 1, stage).start()

    def across(stage):
        if stage == 0:
            y_copy(0, 0, 0).wait_recv()
            c_copy(1, 0, 0).start()
            return
        for way, d, chunk in Z_PARTS:
            if d == stage:
                y_copy(way, d, chunk).wait_recv()
        c_copy(1, 0, stage).start()
        if stage < 4:
            c_copy(1, 1, stage).start()

    def ready(chain, stage):
        c_copy(chain, 0, stage).wait_recv()
        if 0 < stage < 4:
            c_copy(chain, 1, stage).wait_recv()

    def group_step(i, _):
        for when, events in EVENTS.items():
            @pl.when(i == when)
            def _(events=events):
                for event, *at in events:
                    {"near": near, "across": across, "ready": ready, "fine": fine_stage}[event](*at)

        gz, gy = group_of(i)
        first, second = coarse_group(queries[gz, gy], feat, blk * 17)

        @pl.when(i == 0)
        def _():
            stats_in[0, 0] = first
            stats_in[0, 1] = second

        @pl.when(i > 0)
        def _():
            stats_out[i, 0] = first
            stats_out[i, 1] = second
            stat_copy(i).start()

        return 0

    lax.fori_loop(0, PEERS, group_step, 0)

    wait_all(answers.at[1:PEERS], far_recv.at[1])
    wait_all(stats_in.at[1:PEERS], far_recv.at[2])
    coarse_combine(stats_in, out)
    out[8:16, :] = jnp.sum(answers[...], axis=0)

    wait_all(gathered.at[1:PEERS], far_send.at[0])
    wait_all(answers.at[1:PEERS], far_send.at[1])
    wait_all(stats_in.at[1:PEERS], far_send.at[2])
    wait_all(queries.at[0:7, 0, 0:256], near_send.at[0])
    wait_all(queries.at[:, 0, 0:256], near_send.at[1])
    wait_all(queries.at[:, 0, 0:480], near_send.at[2])


def split_result(packed, coarse_pos, offset):
    for i in range(2):
        coarse_pos[i] = packed[4 * i : 4 * i + 4, 0:32]
        offset[i] = packed[8 + 2 * i : 10 + 2 * i, 0:64]


def body(coarse_query, coarse_feat, fine_query, fine_tiles, track_pos, tile_list, tile_valid):
    track_group, heads, channels = coarse_query.shape
    frames_here, region, _ = coarse_feat.shape
    queries = coarse_query.reshape(track_group * heads, channels)
    feat = jnp.transpose(coarse_feat, (1, 0, 2))
    tiles = fine_tiles.reshape(frames_here, -1, fine_tiles.shape[-1])
    pos = jnp.transpose(track_pos, (0, 2, 1))
    lists = jnp.transpose(tile_list[:, 0], (0, 2, 1))
    valid = jnp.transpose(tile_valid[:, 0], (0, 2, 1))
    f32 = jnp.float32
    vmem = pl.BlockSpec(memory_space=pltpu.VMEM)
    far = pl.BlockSpec(memory_space=pl.ANY)
    dma = pltpu.SemaphoreType.DMA
    rows = queries.shape[0]
    packed = pl.pallas_call(
        kernel,
        out_shape=jax.ShapeDtypeStruct((16, 128), f32),
        in_specs=[far, far, far, vmem, vmem, vmem, vmem],
        out_specs=vmem,
        scratch_shapes=[
            pltpu.VMEM((RING, 2, rows, channels), jnp.bfloat16),
            pltpu.VMEM(feat.shape, jnp.bfloat16),
            pltpu.VMEM((region * frames_here, channels), jnp.bfloat16),
            pltpu.VMEM(tiles.shape, jnp.bfloat16),
            pltpu.VMEM((PEERS, 2, 8, rows), f32),
            pltpu.VMEM((PEERS, 2, 8, rows), f32),
            pltpu.VMEM((PEERS, 8, 128), f32),
            pltpu.VMEM((PEERS, 8, 128), f32),
            pltpu.VMEM((PEERS, 8, 128), f32),
            pltpu.VMEM((128, 128), f32),
            pltpu.VMEM((2, 32, 128), f32),
            pltpu.VMEM((32, 32, 128), f32),
            dma((3,)),
            dma((3,)),
            dma((2, 9)),
            dma((2, 8)),
            dma((15,)),
            dma((3,)),
            dma((3,)),
        ],
        compiler_params=pltpu.CompilerParams(
            collective_id=0, has_side_effects=True, vmem_limit_bytes=56 * 2**20
        ),
        cost_estimate=pl.CostEstimate(
            flops=2 * 8192 * 2048 * 256, bytes_accessed=6 * 10**6, transcendentals=8192 * 2048
        ),
    )(queries, feat, tiles, fine_query, pos, lists, valid)
    coarse_pos, offset = pl.pallas_call(
        split_result,
        out_shape=(
            jax.ShapeDtypeStruct((2, 4, 32), f32),
            jax.ShapeDtypeStruct((2, 2, 64), f32),
        ),
        in_specs=[vmem],
        out_specs=(vmem, vmem),
    )(packed)
    return coarse_pos, jnp.transpose(offset, (0, 2, 1))


def solution(mesh):
    return jax.shard_map(
        body,
        mesh=mesh,
        in_specs=(
            P("blk", None, None),
            P("frames", "blk", None),
            P(("blk", "frames"), None),
            P("frames", "blk", None, None),
            P(None, None, ("blk", "frames")),
            P("frames", "blk", None, None),
            P("frames", "blk", None, None),
        ),
        out_specs=(P(None, "frames", "blk"), P(None, None, ("blk", "frames"))),
        check_vma=False,
    )
```
